128 devices in a mesh: feat: 16 (over z, x), dp: 8 (over y, core).
Axes of the slice: x: 4, y: 4, z: 4, core: 2. Of those that a mesh axis runs over, the one named last changes fastest.
Arguments:
- node_table: bfloat16 [768, 65536], P('feat'), may hold values from -6 to 6
- neighbor_ids: int32 [384, 26, 128], P('dp'), may hold values from 0 to 65535
- tile_counts: int32 [128], P(('dp', 'feat')), may hold values from 1 to 3, as said below
- w_self: bfloat16 [768, 1024], P('feat'), may hold values from -0.21875 to 0.21875
- w_neigh: bfloat16 [768, 1024], P('feat'), may hold values from -0.4375 to 0.4375
- bias: float32 [1024], replicated, may hold values from -1 to 1
- cotangent: bfloat16 [384, 128, 1024], P(('dp', 'feat')), may hold values from -6 to 6
Outputs:
- activations: bfloat16 [384, 128, 1024], P(('dp', 'feat'))
- grad_self: float32 [768, 1024], P('feat')
- grad_neigh: float32 [768, 1024], P('feat')
The draws below stay inside these ranges and needn't reach their ends.
Inputs may be any that keep to these rules, and one draw needn't show every extreme that they name: `tile_counts`: some minibatch fills all 3 slots.
All inputs are finite; a program needn't handle non-finite values.
Results may differ from the reference program's by a relative error of at most 0.018.
The reference program's roundings to bfloat16 on the way (of `own`, `mean` and `delta`) count: a program that leaves them out, or rounds other values in their place, can miss the bound.
Values may be sent and summed in bfloat16 or wider, within the bound.
A program may use at most 192 MiB of HBM per device.

```python
import jax
import jax.numpy as jnp
from jax import lax

F = 768
H = 1024
FAN = 25
ROWS = 128
NODES = 65536
TILE_DEV = 3
FAN1 = 26
MINIBATCHES = 128
TILES = 384


def draw_tile_counts(key, part):
    key = jax.random.fold_in(key, 7)
    first, second = jax.random.split(key)
    counts = jax.random.randint(first, (MINIBATCHES,), 1, TILE_DEV + 1)
    place = jax.random.randint(second, (), 0, MINIBATCHES)
    return jnp.where(jnp.arange(MINIBATCHES) == place, TILE_DEV, counts).astype(jnp.int32)


def plant(array, key, low, high):
    spot = [jax.random.randint(jax.random.fold_in(key, axis), (), 0, length) for axis, length in enumerate(array.shape)]
    longest = array.shape.index(max(array.shape))
    neighbour = spot[:longest] + [(spot[longest] + 1) % array.shape[longest]] + spot[longest + 1:]
    return array.at[tuple(spot)].set(low).at[tuple(neighbour)].set(high)


def level_of(stream_key, extent, shards, smallest, high):
    def one(position, shards_of):
        heights = jax.random.uniform(jax.random.fold_in(jax.random.fold_in(stream_key, 6), position), (shards_of,), jnp.float32, smallest / len(shards), high / len(shards))
        return jnp.repeat(jnp.exp(heights), extent[position] // shards_of).reshape((-1,) + (1,) * (len(extent) - position - 1))

    factor_of = one(*shards[0])
    for cut in shards[1:]:
        factor_of = factor_of * one(*cut)
    return factor_of


def noise(key, extent, deviation, most, cuts=(), held_as=jnp.bfloat16):
    gain = level_of(key, extent, cuts, -0.22, 0.18) if cuts else 1.0
    result = jax.random.normal(key, extent, jnp.float32) * deviation * gain
    return jnp.minimum(jnp.maximum(result, -most), most).astype(held_as)


def setup_inputs(seed: int = 0) -> dict:
    streams_of = jax.random.split(jax.random.key(seed), 8)
    return {
        "node_table": noise(streams_of[0], (F, NODES), 1.0, 6.0, ((0, 16),)),
        "neighbor_ids": plant(jax.random.randint(streams_of[1], (TILES, FAN1, ROWS), 0, NODES), jax.random.fold_in(streams_of[1], 1), 0, NODES - 1).astype(jnp.int32),
        "tile_counts": draw_tile_counts(jax.random.fold_in(streams_of[7], 71), 0),
        "w_self": noise(streams_of[3], (F, H), F ** -0.5, 0.21875, ((0, 16),)),
        "w_neigh": noise(streams_of[4], (F, H), (F // 4) ** -0.5, 0.4375, ((0, 16),)),
        "bias": jnp.clip(jax.random.uniform(streams_of[5], (H,), jnp.float32, -1.0, 1.0), -1.0, 1.0),
        "cotangent": noise(streams_of[6], (TILES, ROWS, H), 1.0, 6.0, ((0, 128),)),
    }


def reference(node_table, neighbor_ids, tile_counts, w_self, w_neigh, bias, cotangent):
    slots = jnp.arange(TILES, dtype=jnp.int32)
    live_all = (slots % TILE_DEV) < tile_counts[slots // TILE_DEV]

    def tile_step(carry, inputs):
        ids_tile, cot_tile, live = inputs
        gathered = node_table[:, ids_tile.reshape(-1)].reshape(F, FAN1, ROWS)
        own = gathered[:, 0]
        mean = (jnp.sum(gathered[:, 1:].astype(jnp.float32), axis=1) / FAN).astype(jnp.bfloat16)
        pre = jnp.dot(own.T, w_self, preferred_element_type=jnp.float32)
        pre = pre + jnp.dot(mean.T, w_neigh, preferred_element_type=jnp.float32) + bias
        act = jnp.where(live, jnp.maximum(pre, 0.0), 0.0).astype(jnp.bfloat16)
        delta = jnp.where(live & (pre > 0), cot_tile, jnp.zeros_like(cot_tile))
        grad_a = carry[0] + jnp.dot(own, delta, preferred_element_type=jnp.float32)
        grad_b = carry[1] + jnp.dot(mean, delta, preferred_element_type=jnp.float32)
        return (grad_a, grad_b), act

    start = (jnp.zeros((F, H), jnp.float32), jnp.zeros((F, H), jnp.float32))
    grads, acts = lax.scan(tile_step, start, (neighbor_ids, cotangent, live_all))
    return acts, grads[0], grads[1]
```

```python
import jax
import jax.numpy as jnp
from jax import lax
from jax.experimental import pallas as pl
from jax.experimental.pallas import tpu as pltpu
from jax.sharding import PartitionSpec as P

MESH = pl.DeviceIdType.MESH
UNROLL = 8
BATCH = 8


def gather_kernel(counts, ids_hbm, table, out, nodes, sums, *rest):
    fan = ids_hbm.shape[1]
    ids, sem = (rest[:fan], rest[fan : 2 * fan]), rest[2 * fan]
    block, count = table.shape
    tiles, rows = ids_hbm.shape[0], ids_hbm.shape[2]
    chunk = 512

    def fetch(batch, slot, k):
        return pltpu.make_async_copy(
            ids_hbm.at[pl.ds(batch * BATCH, BATCH), k], ids[slot][k], sem.at[slot, k]
        )

    for k in range(fan):
        fetch(0, 0, k).start()

    def fill(i, carry):
        at = pl.multiple_of(i * chunk, chunk)
        part = table[:, pl.ds(at, chunk)]
        wide = jnp.concatenate([part, part, jnp.zeros((128 - 2 * block, chunk), part.dtype)], 0)
        nodes[pl.ds(at, chunk), :] = wide.T.astype(jnp.float32)
        return carry

    lax.fori_loop(0, count // chunk, fill, 0)
    lane_row = lax.broadcasted_iota(jnp.int32, (1, 128), 1)
    lane = lax.broadcasted_iota(jnp.int32, (rows, 128), 1)

    def one_batch(batch, slot):
        def tile(j, carry):
            t = batch * BATCH + j
            live = lax.rem(t, 3) < counts[lax.div(t, 3)]
            at = pl.multiple_of(lax.rem(t, 3) * rows, rows)

            @pl.when(live)
            def _():
                def group(g, inner):
                    for u in range(UNROLL):
                        r = g * UNROLL + u

                        def node(k):
                            return nodes[pl.ds(ids[slot][k][j, r], 1), :]

                        total = node(1)
                        for k in range(2, fan):
                            total = total + node(k)
                        sums[pl.ds(r, 1), :] = jnp.where(lane_row < block, node(0), total)
                    return inner

                lax.fori_loop(0, rows // UNROLL, group, 0)
                held = sums[...]
                held = jnp.where(lane < block, held, held / (fan - 1.0))
                out[lax.div(t, 3), :, pl.ds(at, rows)] = held.T[: 2 * block].astype(out.dtype)

            @pl.when(jnp.logical_not(live))
            def _():
                out[lax.div(t, 3), :, pl.ds(at, rows)] = jnp.zeros((2 * block, rows), out.dtype)

            return carry

        lax.fori_loop(0, BATCH, tile, 0)

    batches = tiles // BATCH

    def pair(p, carry):
        for slot in range(2):
            batch = p * 2 + slot
            for k in range(fan):
                fetch(batch, slot, k).wait()
            if slot == 0:
                for k in range(fan):
                    fetch(batch + 1, 1, k).start()
            else:

                @pl.when(batch < batches - 1)
                def _():
                    for k in range(fan):
                        fetch(batch + 1, 0, k).start()

            one_batch(batch, slot)
        return carry

    lax.fori_loop(0, batches // 2, pair, 0)


def gather(counts, ids, table):
    tiles, fan, rows = ids.shape
    block, count = table.shape
    owned = 3
    return pl.pallas_call(
        gather_kernel,
        grid_spec=pltpu.PrefetchScalarGridSpec(
            num_scalar_prefetch=1,
            grid=(),
            in_specs=[pl.BlockSpec(memory_space=pl.ANY), pl.BlockSpec(memory_space=pltpu.VMEM)],
            out_specs=pl.BlockSpec(memory_space=pltpu.VMEM),
            scratch_shapes=[
                pltpu.VMEM((count, 128), jnp.float32),
                pltpu.VMEM((rows, 128), jnp.float32),
            ]
            + [pltpu.SMEM((BATCH, rows), jnp.int32)] * (2 * fan)
            + [pltpu.SemaphoreType.DMA((2, fan))],
        ),
        out_shape=jax.ShapeDtypeStruct((tiles // owned, 2 * block, owned * rows), jnp.bfloat16),
        compiler_params=pltpu.CompilerParams(vmem_limit_bytes=56 << 20),
        cost_estimate=pl.CostEstimate(
            flops=120_000_000_000, bytes_accessed=300_000_000, transcendentals=0
        ),
    )(counts, ids, table)


def layer_kernel(
    live_count, x, w, bias, cot, act, out_self, out_neigh,
    mine, turned, delta, other, pair_in, summed, feat_in, y_in, half, half_in,
    x_send, x_recv, p_send, p_recv, f_send, f_recv, y_send, y_recv, h_send, h_recv, local_sem,
):
    f, d = lax.axis_index("feat"), lax.axis_index("dp")
    z, xx = lax.div(f, 4), lax.rem(f, 4)
    y, core = lax.div(d, 2), lax.rem(d, 2)
    partner = {"dp": y * 2 + (1 - core)}
    wide, rows = mine.shape
    two = x.shape[1]
    block = two // 2
    hidden = w.shape[1]
    cols = hidden // 2

    def feat_peer(i, j):
        return lax.rem(z + i, 4) * 4 + lax.rem(xx + j, 4)

    def y_peer(i):
        return {"dp": lax.rem(y + i, 4) * 2 + core}

    others = [(i, j) for i in range(4) for j in range(4) if (i, j) != (0, 0)]

    barrier = pltpu.get_barrier_semaphore()
    for i, j in others:
        pl.semaphore_signal(barrier, inc=1, device_id={"feat": feat_peer(i, j)}, device_id_type=MESH)
    pl.semaphore_signal(barrier, inc=1, device_id=partner, device_id_type=MESH)
    for i in range(1, 4):
        pl.semaphore_signal(barrier, inc=1, device_id=y_peer(i), device_id_type=MESH)
    pl.semaphore_wait(barrier, 19)

    my_rows = pl.ds(pl.multiple_of(f * two, two), two)
    own = pltpu.make_async_copy(x.at[f], mine.at[my_rows], local_sem)
    own.start()
    sends = []
    for i, j in others:
        copy = pltpu.make_async_remote_copy(
            src_ref=x.at[feat_peer(i, j)],
            dst_ref=mine.at[my_rows],
            send_sem=x_send.at[i * 4 + j],
            recv_sem=x_recv.at[i * 4 + j],
            device_id={"feat": feat_peer(i, j)},
            device_id_type=MESH,
        )
        copy.start()
        sends.append(copy)
    own.wait()
    for copy in sends:
        copy.wait()

    def turn(i, carry):
        at = pl.multiple_of(i * 128, 128)
        turned[:, pl.ds(at, 128)] = mine[pl.ds(at, 128), :].T
        return carry

    lax.fori_loop(0, wide // 128, turn, 0)

    tile_rows = rows // 3
    tile_of = lax.div(lax.broadcasted_iota(jnp.int32, (rows, 256), 0), tile_rows)
    live = tile_of < live_count[0]

    def forward(n, carry):
        at = pl.multiple_of(n * 256, 256)
        pre = jnp.dot(turned[...], w[:, pl.ds(at, 256)], preferred_element_type=jnp.float32)
        pre = pre + bias[:, pl.ds(at, 256)]
        on = live & (pre > 0)
        act[:, pl.ds(at, 256)] = jnp.where(on, pre, 0.0).astype(act.dtype)
        c = cot[:, pl.ds(at, 256)].astype(jnp.float32)
        delta[:, pl.ds(at, 256)] = jnp.where(on, c, 0.0).astype(delta.dtype)
        return carry

    lax.fori_loop(0, hidden // 256, forward, 0)

    ours = pl.ds(pl.multiple_of(core * cols, cols), cols)
    theirs = pl.ds(pl.multiple_of((1 - core) * cols, cols), cols)
    group = 4 * two

    def rows_of(i):
        return pl.ds(pl.multiple_of(lax.rem(z + i, 4) * group, group), group)

    order = (1, 2, 3, 0)
    waiting = []
    for i in order:
        other[rows_of(i), :] = jnp.dot(
            mine[rows_of(i), :], delta[:, theirs], preferred_element_type=jnp.float32
        ).astype(other.dtype)
        copy = pltpu.make_async_remote_copy(
            src_ref=other.at[rows_of(i)],
            dst_ref=pair_in.at[rows_of(i)],
            send_sem=p_send.at[i],
            recv_sem=p_recv.at[i],
            device_id=partner,
            device_id_type=MESH,
        )
        copy.start()
        waiting.append(copy)
    out_feat = []
    for i, copy in zip(order, waiting):
        product = jnp.dot(mine[rows_of(i), :], delta[:, ours], preferred_element_type=jnp.float32)
        copy.wait()
        summed[rows_of(i), :] = (product + pair_in[rows_of(i), :].astype(jnp.float32)).astype(
            summed.dtype
        )
        for j in (1, 2, 3, 0):
            if (i, j) == (0, 0):
                continue
            peer = feat_peer(i, j)
            send = pltpu.make_async_remote_copy(
                src_ref=summed.at[pl.ds(pl.multiple_of(peer * two, two), two)],
                dst_ref=feat_in.at[i * 4 + j],
                send_sem=f_send.at[i * 4 + j],
                recv_sem=f_recv.at[i * 4 + j],
                device_id={"feat": peer},
                device_id_type=MESH,
            )
            send.start()
            out_feat.append((i * 4 + j, send))
    total = summed[my_rows, :].astype(jnp.float32)
    for slot, send in out_feat:
        send.wait()
        total = total + feat_in[slot].astype(jnp.float32)
    y_in[y] = total.astype(y_in.dtype)
    out_y = []
    for i in range(1, 4):
        send = pltpu.make_async_remote_copy(
            src_ref=y_in.at[y],
            dst_ref=y_in.at[y],
            send_sem=y_send.at[i],
            recv_sem=y_recv.at[i],
            device_id=y_peer(i),
            device_id_type=MESH,
        )
        send.start()
        out_y.append(send)
    for send in out_y:
        send.wait()
    total = y_in[0].astype(jnp.float32)
    for i in range(1, 4):
        total = total + y_in[i].astype(jnp.float32)
    half[...] = total
    last = pltpu.make_async_remote_copy(
        src_ref=half, dst_ref=half_in, send_sem=h_send, recv_sem=h_recv,
        device_id=partner, device_id_type=MESH,
    )
    last.start()
    out_self[:, ours] = total[:block]
    out_neigh[:, ours] = total[block:]
    last.wait()
    out_self[:, theirs] = half_in[:block]
    out_neigh[:, theirs] = half_in[block:]


def layer(count, x, w, bias, cot):
    peers, two, rows = x.shape
    wide, hidden = w.shape
    block, cols = two // 2, hidden // 2
    bf16, f32 = jnp.bfloat16, jnp.float32
    vmem = pl.BlockSpec(memory_space=pltpu.VMEM)
    dma = pltpu.SemaphoreType.DMA
    return pl.pallas_call(
        layer_kernel,
        in_specs=[
            pl.BlockSpec(memory_space=pltpu.SMEM),
            pl.BlockSpec(memory_space=pl.ANY),
            vmem, vmem, vmem,
        ],
        out_specs=[vmem, vmem, vmem],
        out_shape=[
            jax.ShapeDtypeStruct((rows, hidden), bf16),
            jax.ShapeDtypeStruct((block, hidden), f32),
            jax.ShapeDtypeStruct((block, hidden), f32),
        ],
        scratch_shapes=[
            pltpu.VMEM((wide, rows), bf16),
            pltpu.VMEM((rows, wide), bf16),
            pltpu.VMEM((rows, hidden), bf16),
            pltpu.VMEM((wide, cols), bf16),
            pltpu.VMEM((wide, cols), bf16),
            pltpu.VMEM((wide, cols), bf16),
            pltpu.VMEM((peers, two, cols), bf16),
            pltpu.VMEM((4, two, cols), bf16),
            pltpu.VMEM((two, cols), f32),
            pltpu.VMEM((two, cols), f32),
            dma((16,)), dma((16,)), dma((4,)), dma((4,)), dma((16,)), dma((16,)),
            dma((4,)), dma((4,)), dma, dma, dma,
        ],
        compiler_params=pltpu.CompilerParams(
            collective_id=0, has_side_effects=True, vmem_limit_bytes=56 << 20
        ),
        cost_estimate=pl.CostEstimate(
            flops=2_500_000_000, bytes_accessed=10_000_000, transcendentals=0
        ),
    )(count, x, w, bias, cot)


def local(node_table, neighbor_ids, tile_counts, w_self, w_neigh, bias, cotangent):
    owned, rows, hidden = cotangent.shape
    counts = lax.all_gather(tile_counts, "feat", axis=0, tiled=True)
    w = lax.all_gather(jnp.concatenate([w_self, w_neigh], 0), "feat", axis=0, tiled=True)
    x = gather(counts, neighbor_ids, node_table)
    act, grad_self, grad_neigh = layer(
        tile_counts, x, w, bias.reshape(1, hidden), cotangent.reshape(owned * rows, hidden)
    )
    return act.reshape(owned, rows, hidden), grad_self, grad_neigh


def solution(mesh):
    return jax.shard_map(
        local,
        mesh=mesh,
        in_specs=(
            P("feat", None),
            P("dp", None, None),
            P(("dp", "feat")),
            P("feat", None),
            P("feat", None),
            P(),
            P(("dp", "feat"), None, None),
        ),
        out_specs=(P(("dp", "feat"), None, None), P("feat", None), P("feat", None)),
        check_vma=False,
    )
```

```python
import jax
import jax.numpy as jnp
from jax import lax
from jax.experimental import pallas as pl
from jax.experimental.pallas import tpu as pltpu
from jax.sharding import PartitionSpec as P

MESH = pl.DeviceIdType.MESH
UNROLL = 16
BATCH = 8
CHUNK = 2048
LOADS = 8


def gather_kernel(counts, ids_hbm, table_hbm, out, nodes, sums, table, load_sem, *rest):
    fan, tiles, rows = ids_hbm.shape
    ids, sem = (rest[:fan], rest[fan : 2 * fan]), rest[2 * fan]
    block, count = table_hbm.shape
    piece = count // LOADS

    def load(i):
        at = pl.ds(pl.multiple_of(i * piece, piece), piece)
        return pltpu.make_async_copy(table_hbm.at[:, at], table.at[:, at], load_sem.at[i])

    for i in range(LOADS):
        load(i).start()

    def fetch(batch, slot, k):
        return pltpu.make_async_copy(
            ids_hbm.at[k, pl.ds(batch * BATCH, BATCH)], ids[slot][k], sem.at[slot, k]
        )

    for k in range(fan):
        fetch(0, 0, k).start()

    def fill(i, carry):
        load(i).wait()

        def turn(j, inner):
            at = pl.multiple_of(i * piece + j * CHUNK, CHUNK)
            part = table[:, pl.ds(at, CHUNK)]
            wide = jnp.concatenate([part, part, jnp.zeros((128 - 2 * block, CHUNK), part.dtype)], 0)
            nodes[pl.ds(at, CHUNK), :] = wide.T.astype(jnp.float32)
            return inner

        lax.fori_loop(0, piece // CHUNK, turn, 0)
        return carry

    lax.fori_loop(0, LOADS, fill, 0)
    lane_row = lax.broadcasted_iota(jnp.int32, (1, 128), 1)
    lane = lax.broadcasted_iota(jnp.int32, (rows, 128), 1)

    def one_batch(batch, slot):
        def tile(j, carry):
            t = batch * BATCH + j
            live = lax.rem(t, 3) < counts[lax.div(t, 3), 0, 0]
            at = pl.multiple_of(lax.rem(t, 3) * rows, rows)

            @pl.when(live)
            def _():
                def group(g, inner):
                    for u in range(UNROLL):
                        r = g * UNROLL + u

                        def node(k):
                            return nodes[pl.ds(ids[slot][k][j, r], 1), :]

                        total = node(1)
                        for k in range(2, fan):
                            total = total + node(k)
                        sums[pl.ds(r, 1), :] = jnp.where(lane_row < block, node(0), total)
                    return inner

                lax.fori_loop(0, rows // UNROLL, group, 0)
                held = sums[...]
                held = jnp.where(lane < block, held, held / (fan - 1.0))
                turned = held.T.astype(out.dtype)
                out[lax.div(t, 3), 0, :, pl.ds(at, rows)] = turned[:block]
                out[lax.div(t, 3), 1, :, pl.ds(at, rows)] = turned[block : 2 * block]

            @pl.when(jnp.logical_not(live))
            def _():
                out[lax.div(t, 3), :, :, pl.ds(at, rows)] = jnp.zeros((2, block, rows), out.dtype)

            return carry

        lax.fori_loop(0, BATCH, tile, 0)

    batches = tiles // BATCH

    def pair(p, carry):
        for slot in range(2):
            batch = p * 2 + slot
            for k in range(fan):
                fetch(batch, slot, k).wait()
            if slot == 0:
                for k in range(fan):
                    fetch(batch + 1, 1, k).start()
            else:

                @pl.when(batch < batches - 1)
                def _():
                    for k in range(fan):
                        fetch(batch + 1, 0, k).start()

            one_batch(batch, slot)
        return carry

    lax.fori_loop(0, batches // 2, pair, 0)


def gather(counts, ids, table):
    fan, tiles, rows = ids.shape
    block, count = table.shape
    owned = 3
    return pl.pallas_call(
        gather_kernel,
        in_specs=[
            pl.BlockSpec(memory_space=pltpu.SMEM),
            pl.BlockSpec(memory_space=pl.ANY),
            pl.BlockSpec(memory_space=pl.ANY),
        ],
        out_specs=pl.BlockSpec(memory_space=pltpu.VMEM),
        scratch_shapes=[
            pltpu.VMEM((count, 128), jnp.float32),
            pltpu.VMEM((rows, 128), jnp.float32),
            pltpu.VMEM((block, count), table.dtype),
            pltpu.SemaphoreType.DMA((LOADS,)),
        ]
        + [pltpu.SMEM((BATCH, rows), jnp.int32)] * (2 * fan)
        + [pltpu.SemaphoreType.DMA((2, fan))],
        out_shape=jax.ShapeDtypeStruct((tiles // owned, 2, block, owned * rows), jnp.bfloat16),
        compiler_params=pltpu.CompilerParams(vmem_limit_bytes=56 << 20),
        cost_estimate=pl.CostEstimate(
            flops=120_000_000_000, bytes_accessed=300_000_000, transcendentals=0
        ),
    )(counts, ids, table)


def count_kernel(count, out, got, send_sem, recv_sem):
    f = lax.axis_index("feat")
    peers = out.shape[0]
    barrier = pltpu.get_barrier_semaphore()
    for i in range(1, peers):
        pl.semaphore_signal(
            barrier, inc=1, device_id={"feat": lax.rem(f + i, peers)}, device_id_type=MESH
        )
    got[f] = jnp.zeros(got.shape[1:], jnp.int32) + count[0]
    pl.semaphore_wait(barrier, peers - 1)
    copies = []
    for i in range(1, peers):
        copy = pltpu.make_async_remote_copy(
            src_ref=got.at[f],
            dst_ref=got.at[f],
            send_sem=send_sem.at[i],
            recv_sem=recv_sem.at[i],
            device_id={"feat": lax.rem(f + i, peers)},
            device_id_type=MESH,
        )
        copy.start()
        copies.append(copy)
    for copy in copies:
        copy.wait()
    out[...] = got[...]


def exchange_counts(count):
    peers = 16
    return pl.pallas_call(
        count_kernel,
        in_specs=[pl.BlockSpec(memory_space=pltpu.SMEM)],
        out_specs=pl.BlockSpec(memory_space=pltpu.VMEM),
        out_shape=jax.ShapeDtypeStruct((peers, 1, 128), jnp.int32),
        scratch_shapes=[
            pltpu.VMEM((peers, 1, 128), jnp.int32),
            pltpu.SemaphoreType.DMA((peers,)),
            pltpu.SemaphoreType.DMA((peers,)),
        ],
        compiler_params=pltpu.CompilerParams(collective_id=1, has_side_effects=True),
    )(count)


def finish_kernel(a, b, c, out_a, out_b, out_c, sem):
    copies = [
        pltpu.make_async_copy(x, y, sem.at[i])
        for i, (x, y) in enumerate(((a, out_a), (b, out_b), (c, out_c)))
    ]
    for copy in copies:
        copy.start()
    for copy in copies:
        copy.wait()


def finish(*arrays):
    return pl.pallas_call(
        finish_kernel,
        in_specs=[pl.BlockSpec(memory_space=pl.ANY)] * 3,
        out_specs=[pl.BlockSpec(memory_space=pl.ANY)] * 3,
        out_shape=[jax.ShapeDtypeStruct(x.shape, x.dtype) for x in arrays],
        scratch_shapes=[pltpu.SemaphoreType.DMA((3,))],
        compiler_params=pltpu.CompilerParams(vmem_limit_bytes=56 << 20),
    )(*arrays)


def layer_kernel(
    live_count, x, w_self, w_neigh, bias, cot, act, out_self, out_neigh,
    w, mine, turned, delta, other, pair_in, part_a, relay_a, in_a, part_b, relay_b, in_b,
    y_out, y_in, half, half_in, x_send, x_recv, p_send, p_recv, r_send, r_recv, y_send, y_recv, h_send, h_recv, local_sem, w_sem,
):
    f, d = lax.axis_index("feat"), lax.axis_index("dp")
    z, xx = lax.div(f, 4), lax.rem(f, 4)
    y, core = lax.div(d, 2), lax.rem(d, 2)
    partner = {"dp": y * 2 + (1 - core)}
    half_wide, rows = mine.shape[1:]
    block = x.shape[2]
    hidden = w.shape[1]
    cols = hidden // 2

    def feat_peer(i, j):
        return lax.rem(z + i, 4) * 4 + lax.rem(xx + j, 4)

    others = [(i, j) for i in range(4) for j in range(4) if (i, j) != (0, 0)]

    weights = [
        pltpu.make_async_copy(part, w.at[pl.ds(p * half_wide, half_wide)], w_sem.at[p])
        for p, part in enumerate((w_self, w_neigh))
    ]
    for copy in weights:
        copy.start()

    barrier = pltpu.get_barrier_semaphore()
    for i, j in others:
        pl.semaphore_signal(barrier, inc=1, device_id={"feat": feat_peer(i, j)}, device_id_type=MESH)
    pl.semaphore_signal(barrier, inc=1, device_id=partner, device_id_type=MESH)
    for at in (y + 1 - 2 * lax.rem(y, 2), 3 - y):
        pl.semaphore_signal(barrier, inc=1, device_id={"dp": at * 2 + core}, device_id_type=MESH)
    pl.semaphore_wait(barrier, 18)

    my_rows = pl.ds(pl.multiple_of(f * block, block), block)
    own = pltpu.make_async_copy(x.at[f], mine.at[:, my_rows], local_sem)
    own.start()
    sends = []
    for i, j in others:
        copy = pltpu.make_async_remote_copy(
            src_ref=x.at[feat_peer(i, j)],
            dst_ref=mine.at[:, my_rows],
            send_sem=x_send.at[i * 4 + j],
            recv_sem=x_recv.at[i * 4 + j],
            device_id={"feat": feat_peer(i, j)},
            device_id_type=MESH,
        )
        copy.start()
        sends.append(copy)
    own.wait()
    for copy in sends:
        copy.wait()

    def turn(i, carry):
        at = pl.multiple_of(i * 128, 128)
        for p in range(2):
            to = pl.multiple_of(p * half_wide + i * 128, 128)
            turned[:, pl.ds(to, 128)] = mine[p, pl.ds(at, 128), :].T
        return carry

    lax.fori_loop(0, half_wide // 128, turn, 0)
    for copy in weights:
        copy.wait()

    tile_rows = rows // 3
    tile_of = lax.div(lax.broadcasted_iota(jnp.int32, (rows, 256), 0), tile_rows)
    live = tile_of < live_count[0]

    def forward(n, carry):
        at = pl.multiple_of(n * 256, 256)
        pre = jnp.dot(turned[...], w[:, pl.ds(at, 256)], preferred_element_type=jnp.float32)
        pre = pre + bias[:, pl.ds(at, 256)]
        on = live & (pre > 0)
        act[:, pl.ds(at, 256)] = jnp.where(on, pre, 0.0).astype(act.dtype)
        c = cot[:, pl.ds(at, 256)].astype(jnp.float32)
        delta[:, pl.ds(at, 256)] = jnp.where(on, c, 0.0).astype(delta.dtype)
        return carry

    lax.fori_loop(0, hidden // 256, forward, 0)

    quarter = cols // 2

    def ours(h):
        return pl.ds(pl.multiple_of(core * cols + h * quarter, quarter), quarter)

    def theirs(h):
        return pl.ds(pl.multiple_of((1 - core) * cols + h * quarter, quarter), quarter)

    def product(p, at):
        return jnp.dot(mine[p], delta[:, at], preferred_element_type=jnp.float32)

    def remote(src, dst, send_sem, recv_sem, peer):
        copy = pltpu.make_async_remote_copy(
            src_ref=src, dst_ref=dst, send_sem=send_sem, recv_sem=recv_sem,
            device_id=peer, device_id_type=MESH,
        )
        copy.start()
        return copy

    def place(h, phase):
        return xx if (h + phase) % 2 == 0 else z

    def neighbour(h, phase, s):
        at = lax.rem(place(h, phase) + 4 + s, 4)
        return {"feat": z * 4 + at if (h + phase) % 2 == 0 else at * 4 + xx}

    phases = ((part_a, relay_a, in_a), (part_b, relay_b, in_b))
    started = {}

    def ring(h, phase, messages):
        part, relay, arrived = (buffer.at[h] for buffer in phases[phase])
        pos = place(h, phase)
        far, after, before = (lax.rem(pos + s, 4) for s in (2, 1, 3))
        plan = (
            (1, part.at[far, 0], relay.at[0]),
            (-1, part.at[far, 1], relay.at[1]),
            (1, part.at[after, 1], arrived.at[0, 1]),
            (-1, part.at[before, 0], arrived.at[1, 0]),
            (1, part.at[after, 0], arrived.at[0, 0]),
            (-1, part.at[before, 1], arrived.at[1, 1]),
        )
        for m in messages:
            step, src, dst = plan[m]
            started[h, phase, m] = remote(
                src, dst, r_send.at[phase, h, m], r_recv.at[phase, h, m], neighbour(h, phase, step)
            )

    def pass_on(h, phase):
        part, relay, _ = (buffer.at[h] for buffer in phases[phase])
        pos = place(h, phase)
        for way, step in ((0, 1), (1, 3)):
            at = lax.rem(pos + step, 4)
            started[h, phase, way].wait_recv()
            part[at, way] = (
                part[at, way].astype(jnp.float32) + relay[way].astype(jnp.float32)
            ).astype(part.dtype)
            ring(h, phase, (4 + way,))

    def gathered(h, phase, p):
        part, _, arrived = (buffer.at[h] for buffer in phases[phase])
        for m in ((4, 3), (2, 5))[p]:
            started[h, phase, m].wait_recv()
        return (
            part[place(h, phase), p].astype(jnp.float32)
            + arrived[0, p].astype(jnp.float32)
            + arrived[1, p].astype(jnp.float32)
        )

    order = ((0, 0), (0, 1), (1, 0), (1, 1))
    pairs = []
    for q, (h, p) in enumerate(order):
        other[q] = product(p, theirs(h)).astype(other.dtype)
        pairs.append(remote(other.at[q], pair_in.at[q], p_send.at[q], p_recv.at[q], partner))
    for q, (h, p) in enumerate(order):
        own_part = product(p, ours(h))
        pairs[q].wait_recv()
        own_part = (own_part + pair_in[q].astype(jnp.float32)).astype(part_a.dtype)
        for i in range(4):
            for j in range(4):
                rows_ij = own_part[(i * 4 + j) * block : (i * 4 + j + 1) * block]
                if h == 0:
                    part_a[h, j, p, i] = rows_ij
                else:
                    part_a[h, i, p, j] = rows_ij
        ring(h, 0, (0, 3) if p == 0 else (1, 2))
        if q >= 2:
            pass_on(q - 2, 0)
    for h in range(2):
        for p in range(2):
            reduced = gathered(h, 0, p).astype(part_b.dtype)
            for i in range(4):
                part_b[h, i, p] = reduced[i]
            ring(h, 1, (0, 3) if p == 0 else (1, 2))
    for h in range(2):
        pass_on(h, 1)

    def y_peer_of(h, stage):
        at = y + 1 - 2 * lax.rem(y, 2) if (h + stage) % 2 == 0 else 3 - y
        return {"dp": at * 2 + core}

    across = {}
    for h in range(2):
        for p in range(2):
            y_out[h, 0, p] = gathered(h, 1, p).astype(y_out.dtype)
        across[h, 0] = remote(
            y_out.at[h, 0], y_in.at[h, 0], y_send.at[h, 0], y_recv.at[h, 0], y_peer_of(h, 0)
        )
    for h in range(2):
        across[h, 0].wait_recv()
        both = y_out[h, 0].astype(jnp.float32) + y_in[h, 0].astype(jnp.float32)
        y_out[h, 1] = both.astype(y_out.dtype)
        across[h, 1] = remote(
            y_out.at[h, 1], y_in.at[h, 1], y_send.at[h, 1], y_recv.at[h, 1], y_peer_of(h, 1)
        )
    last = []
    for h in range(2):
        across[h, 1].wait_recv()
        half[h] = y_out[h, 1].astype(jnp.float32) + y_in[h, 1].astype(jnp.float32)
        last.append(remote(half.at[h], half_in.at[h], h_send.at[h], h_recv.at[h], partner))
        out_self[:, ours(h)] = half[h, 0]
        out_neigh[:, ours(h)] = half[h, 1]
    for h in range(2):
        last[h].wait_recv()
        out_self[:, theirs(h)] = half_in[h, 0]
        out_neigh[:, theirs(h)] = half_in[h, 1]
    for copy in [*pairs, *started.values(), *across.values(), *last]:
        copy.wait_send()


def layer(count, x, w_self, w_neigh, bias, cot):
    peers, _, block, rows = x.shape
    half_wide, hidden = w_self.shape
    quarter = hidden // 4
    bf16, f32 = jnp.bfloat16, jnp.float32
    vmem = pl.BlockSpec(memory_space=pltpu.VMEM)
    hbm = pl.BlockSpec(memory_space=pl.ANY)
    dma = pltpu.SemaphoreType.DMA
    return pl.pallas_call(
        layer_kernel,
        in_specs=[pl.BlockSpec(memory_space=pltpu.SMEM), hbm, hbm, hbm, vmem, vmem],
        out_specs=[vmem, vmem, vmem],
        out_shape=[
            jax.ShapeDtypeStruct((rows, hidden), bf16),
            jax.ShapeDtypeStruct((block, hidden), f32),
            jax.ShapeDtypeStruct((block, hidden), f32),
        ],
        scratch_shapes=[
            pltpu.VMEM((2 * half_wide, hidden), bf16),
            pltpu.VMEM((2, half_wide, rows), bf16),
            pltpu.VMEM((rows, 2 * half_wide), bf16),
            pltpu.VMEM((rows, hidden), bf16),
            pltpu.VMEM((4, half_wide, quarter), bf16),
            pltpu.VMEM((4, half_wide, quarter), bf16),
            pltpu.VMEM((2, 4, 2, 4, block, quarter), bf16),
            pltpu.VMEM((2, 2, 4, block, quarter), bf16),
            pltpu.VMEM((2, 2, 2, 4, block, quarter), bf16),
            pltpu.VMEM((2, 4, 2, block, quarter), bf16),
            pltpu.VMEM((2, 2, block, quarter), bf16),
            pltpu.VMEM((2, 2, 2, block, quarter), bf16),
            pltpu.VMEM((2, 2, 2, block, quarter), bf16),
            pltpu.VMEM((2, 2, 2, block, quarter), bf16),
            pltpu.VMEM((2, 2, block, quarter), f32),
            pltpu.VMEM((2, 2, block, quarter), f32),
            dma((16,)), dma((16,)), dma((4,)), dma((4,)), dma((2, 2, 6)), dma((2, 2, 6)),
            dma((2, 2)), dma((2, 2)), dma((2,)), dma((2,)), dma, dma((2,)),
        ],
        compiler_params=pltpu.CompilerParams(
            collective_id=0, has_side_effects=True, vmem_limit_bytes=56 << 20
        ),
        cost_estimate=pl.CostEstimate(
            flops=2_500_000_000, bytes_accessed=10_000_000, transcendentals=0
        ),
    )(count, x, w_self, w_neigh, bias, cot)


def local(node_table, neighbor_ids, tile_counts, w_self, w_neigh, bias, cotangent):
    owned, rows, hidden = cotangent.shape
    w_self_all = lax.all_gather(w_self, "feat", axis=0, tiled=True)
    w_neigh_all = lax.all_gather(w_neigh, "feat", axis=0, tiled=True)
    x = gather(exchange_counts(tile_counts), neighbor_ids.transpose(1, 0, 2), node_table)
    act, grad_self, grad_neigh = layer(
        tile_counts,
        x,
        w_self_all,
        w_neigh_all,
        bias.reshape(1, hidden),
        cotangent.reshape(owned * rows, hidden),
    )
    act, grad_self, grad_neigh = finish(act, grad_self, grad_neigh)
    return act.reshape(owned, rows, hidden), grad_self, grad_neigh


def solution(mesh):
    return jax.shard_map(
        local,
        mesh=mesh,
        in_specs=(
            P("feat", None),
            P("dp", None, None),
            P(("dp", "feat")),
            P("feat", None),
            P("feat", None),
            P(),
            P(("dp", "feat"), None, None),
        ),
        out_specs=(P(("dp", "feat"), None, None), P("feat", None), P("feat", None)),
        check_vma=False,
    )
```

```python
import jax
import jax.numpy as jnp
from jax import lax
from jax.experimental import pallas as pl
from jax.experimental.pallas import tpu as pltpu
from jax.sharding import PartitionSpec as P

MESH = pl.DeviceIdType.MESH
UNROLL = 16
BATCH = 8
CHUNK = 2048
LOADS = 8


def tile_sums(nodes, sums, ids, rows, block, base):
    lane_row = lax.broadcasted_iota(jnp.int32, (1, 128), 1)

    def group(g, carry):
        for u in range(UNROLL):
            r = g * UNROLL + u

            def node(k):
                return nodes[pl.ds(ids[k][base + r], 1), :]

            total = node(1)
            for k in range(2, len(ids)):
                total = total + node(k)
            sums[pl.ds(r, 1), :] = jnp.where(lane_row < block, node(0), total)
        return carry

    lax.fori_loop(0, rows // UNROLL, group, 0)
    held = sums[...]
    lane = lax.broadcasted_iota(jnp.int32, held.shape, 1)
    held = jnp.where(lane < block, held, held / (len(ids) - 1.0))
    return held.T.astype(jnp.bfloat16)


def first_kernel(
    count, ids_hbm, table_hbm, nodes, counts, first, table, sums, sent, landed, got, *rest
):
    fan, _, rows = ids_hbm.shape
    ids = (rest[:fan], rest[fan : 2 * fan])
    ids_sem, load_sem, c_send, c_recv, x_send, x_recv = rest[2 * fan :]
    block, width = table_hbm.shape
    peers = got.shape[0]
    f = lax.axis_index("feat")
    piece = width // LOADS

    def load(i):
        at = pl.ds(pl.multiple_of(i * piece, piece), piece)
        return pltpu.make_async_copy(table_hbm.at[:, at], table.at[:, at], load_sem.at[i])

    def peer(i):
        return lax.rem(f + i, peers)

    def fetch(i, slot, k):
        return pltpu.make_async_copy(
            ids_hbm.at[k, peer(i) * 3], ids[slot][k], ids_sem.at[slot, k]
        )

    for i in range(LOADS):
        load(i).start()
    for k in range(fan):
        fetch(1, 0, k).start()
    barrier = pltpu.get_barrier_semaphore()
    for i in range(1, peers):
        pl.semaphore_signal(barrier, inc=1, device_id={"feat": peer(i)}, device_id_type=MESH)
    got[f] = jnp.zeros(got.shape[1:], jnp.int32) + count[0]

    def fill(i, carry):
        load(i).wait()

        def turn(j, inner):
            at = pl.multiple_of(i * piece + j * CHUNK, CHUNK)
            part = table[:, pl.ds(at, CHUNK)]
            wide = jnp.concatenate([part, part, jnp.zeros((128 - 2 * block, CHUNK), part.dtype)], 0)
            nodes[pl.ds(at, CHUNK), :] = wide.T.astype(jnp.float32)
            return inner

        lax.fori_loop(0, piece // CHUNK, turn, 0)
        return carry

    lax.fori_loop(0, LOADS, fill, 0)
    pl.semaphore_wait(barrier, peers - 1)

    def count_copy(i):
        return pltpu.make_async_remote_copy(
            src_ref=got.at[f], dst_ref=got.at[f], send_sem=c_send.at[i], recv_sem=c_recv.at[i],
            device_id={"feat": peer(i)}, device_id_type=MESH,
        )

    my_rows = pl.ds(pl.multiple_of(f * block, block), block)

    def tile_copy(i):
        return pltpu.make_async_remote_copy(
            src_ref=sent.at[peer(i)], dst_ref=landed.at[:, my_rows],
            send_sem=x_send.at[i], recv_sem=x_recv.at[i],
            device_id={"feat": peer(i)}, device_id_type=MESH,
        )

    for i in range(1, peers):
        count_copy(i).start()

    def pair(p, carry):
        for slot in range(2):
            i = p * 2 + slot + 1
            for k in range(fan):
                fetch(i, slot, k).wait()
            if slot == 0:
                for k in range(fan):
                    fetch(i + 1, 1, k).start()
            else:

                @pl.when(i < peers)
                def _():
                    for k in range(fan):
                        fetch(i + 1, 0, k).start()

            turned = tile_sums(nodes, sums, ids[slot], rows, block, 0)
            for part in range(2):
                sent[peer(i), part] = turned[part * block : (part + 1) * block]

            @pl.when(i < peers)
            def _():
                tile_copy(i).start()

        return carry

    lax.fori_loop(0, peers // 2, pair, 0)
    for part in range(2):
        landed[part, my_rows] = sent[f, part]

    def settle(i, carry):
        count_copy(i).wait()
        tile_copy(i).wait()
        return carry

    lax.fori_loop(1, peers, settle, 0)
    counts[...] = got[...]
    first[...] = landed[...]


def first_tiles(count, ids, table):
    fan, tiles, rows = ids.shape
    block, width = table.shape
    peers = tiles // 3
    dma = pltpu.SemaphoreType.DMA
    hbm = pl.BlockSpec(memory_space=pl.ANY)
    vmem = pl.BlockSpec(memory_space=pltpu.VMEM)
    nodes, counts, first = pl.pallas_call(
        first_kernel,
        in_specs=[pl.BlockSpec(memory_space=pltpu.SMEM), hbm, hbm],
        out_specs=[vmem, vmem, vmem],
        out_shape=[
            pltpu.VMEM((width, 128), jnp.float32),
            jax.ShapeDtypeStruct((peers, 1, 128), jnp.int32),
            jax.ShapeDtypeStruct((2, peers * block, rows), jnp.bfloat16),
        ],
        scratch_shapes=[
            pltpu.VMEM((block, width), table.dtype),
            pltpu.VMEM((rows, 128), jnp.float32),
            pltpu.VMEM((peers, 2, block, rows), jnp.bfloat16),
            pltpu.VMEM((2, peers * block, rows), jnp.bfloat16),
            pltpu.VMEM((peers, 1, 128), jnp.int32),
        ]
        + [pltpu.SMEM((rows,), jnp.int32)] * (2 * fan)
        + [dma((2, fan)), dma((LOADS,)), dma((peers,)), dma((peers,)), dma((peers,)), dma((peers,))],
        compiler_params=pltpu.CompilerParams(
            collective_id=1, has_side_effects=True, vmem_limit_bytes=16 << 20
        ),
        cost_estimate=pl.CostEstimate(
            flops=60_000_000_000, bytes_accessed=150_000_000, transcendentals=0
        ),
    )(count, ids, table)
    return pltpu.with_memory_space_constraint(nodes, pltpu.VMEM), counts, first


def gather_kernel(counts, ids_hbm, nodes, out, sums, *rest):
    fan, tiles, rows = ids_hbm.shape
    ids, sem = (rest[:fan], rest[fan : 2 * fan]), rest[2 * fan]
    block = out.shape[2]
    flat = [[ref.reshape(BATCH * rows) for ref in refs] for refs in ids]

    def fetch(batch, slot, k):
        return pltpu.make_async_copy(
            ids_hbm.at[k, pl.ds(batch * BATCH, BATCH)], ids[slot][k], sem.at[slot, k]
        )

    for k in range(fan):
        fetch(0, 0, k).start()

    def one_batch(batch, slot):
        def tile(j, carry):
            t = batch * BATCH + j
            m, place = lax.div(t, 3), lax.rem(t, 3)
            live = place < counts[m, 0, 0]
            at = pl.ds(pl.multiple_of(jnp.maximum(place - 1, 0) * rows, rows), rows)

            @pl.when(live & (place > 0))
            def _():
                turned = tile_sums(nodes, sums, flat[slot], rows, block, j * rows)
                out[m, 0, :, at] = turned[:block]
                out[m, 1, :, at] = turned[block : 2 * block]

            @pl.when(jnp.logical_not(live))
            def _():
                out[m, :, :, at] = jnp.zeros((2, block, rows), out.dtype)

            return carry

        lax.fori_loop(0, BATCH, tile, 0)

    batches = tiles // BATCH

    def pair(p, carry):
        for slot in range(2):
            batch = p * 2 + slot
            for k in range(fan):
                fetch(batch, slot, k).wait()
            if slot == 0:
                for k in range(fan):
                    fetch(batch + 1, 1, k).start()
            else:

                @pl.when(batch < batches - 1)
                def _():
                    for k in range(fan):
                        fetch(batch + 1, 0, k).start()

            one_batch(batch, slot)
        return carry

    lax.fori_loop(0, batches // 2, pair, 0)


def gather(counts, ids, nodes, block):
    fan, tiles, rows = ids.shape
    vmem = pl.BlockSpec(memory_space=pltpu.VMEM)
    return pl.pallas_call(
        gather_kernel,
        in_specs=[pl.BlockSpec(memory_space=pltpu.SMEM), pl.BlockSpec(memory_space=pl.ANY), vmem],
        out_specs=vmem,
        scratch_shapes=[pltpu.VMEM((rows, 128), jnp.float32)]
        + [pltpu.SMEM((BATCH, rows), jnp.int32)] * (2 * fan)
        + [pltpu.SemaphoreType.DMA((2, fan))],
        out_shape=jax.ShapeDtypeStruct((tiles // 3, 2, block, 2 * rows), jnp.bfloat16),
        compiler_params=pltpu.CompilerParams(vmem_limit_bytes=16 << 20),
        cost_estimate=pl.CostEstimate(
            flops=60_000_000_000, bytes_accessed=150_000_000, transcendentals=0
        ),
    )(counts, ids, nodes)


def finish_kernel(a, b, c, out_a, out_b, out_c, held_a, held_b, held_c, sem):
    moves = []
    for q in range(4):
        at = pl.ds(q * (a.shape[0] // 4), a.shape[0] // 4)
        moves.append((a.at[at], held_a.at[at], out_a.at[at]))
    moves += [(b, held_b, out_b), (c, held_c, out_c)]
    ins = [pltpu.make_async_copy(x, h, sem.at[0, i]) for i, (x, h, _) in enumerate(moves)]
    outs = [pltpu.make_async_copy(h, o, sem.at[1, i]) for i, (_, h, o) in enumerate(moves)]
    for copy in ins:
        copy.start()
    for arrived, leaving in zip(ins, outs):
        arrived.wait()
        leaving.start()
    for copy in outs:
        copy.wait()


def finish(*arrays):
    return pl.pallas_call(
        finish_kernel,
        in_specs=[pl.BlockSpec(memory_space=pl.ANY)] * 3,
        out_specs=[pl.BlockSpec(memory_space=pl.ANY)] * 3,
        out_shape=[jax.ShapeDtypeStruct(x.shape, x.dtype) for x in arrays],
        scratch_shapes=[pltpu.VMEM(x.shape, x.dtype) for x in arrays]
        + [pltpu.SemaphoreType.DMA((2, 6))],
        compiler_params=pltpu.CompilerParams(vmem_limit_bytes=56 << 20),
    )(*arrays)


def layer_kernel(
    live_count, first, x, w_self, w_neigh, bias, cot, act, out_self, out_neigh,
    w, mine, turned, delta, other, pair_in, part_a, relay_a, in_a, part_b, relay_b, in_b,
    y_out, y_in, half, half_in, x_send, x_recv, p_send, p_recv, r_send, r_recv, y_send, y_recv, h_send, h_recv, local_sem, w_sem,
):
    f, d = lax.axis_index("feat"), lax.axis_index("dp")
    z, xx = lax.div(f, 4), lax.rem(f, 4)
    y, core = lax.div(d, 2), lax.rem(d, 2)
    partner = {"dp": y * 2 + (1 - core)}
    half_wide, rows = mine.shape[1:]
    block = x.shape[2]
    hidden = w.shape[1]
    cols = hidden // 2

    def feat_peer(i, j):
        return lax.rem(z + i, 4) * 4 + lax.rem(xx + j, 4)

    others = [(i, j) for i in range(4) for j in range(4) if (i, j) != (0, 0)]

    weights = [
        pltpu.make_async_copy(part, w.at[pl.ds(p * half_wide, half_wide)], w_sem.at[p])
        for p, part in enumerate((w_self, w_neigh))
    ]
    for copy in weights:
        copy.start()

    barrier = pltpu.get_barrier_semaphore()
    for i, j in others:
        pl.semaphore_signal(barrier, inc=1, device_id={"feat": feat_peer(i, j)}, device_id_type=MESH)
    pl.semaphore_signal(barrier, inc=1, device_id=partner, device_id_type=MESH)
    for at in (y + 1 - 2 * lax.rem(y, 2), 3 - y):
        pl.semaphore_signal(barrier, inc=1, device_id={"dp": at * 2 + core}, device_id_type=MESH)
    pl.semaphore_wait(barrier, 18)

    tile_rows = rows // 3
    early = pltpu.make_async_copy(first, mine.at[:, :, pl.ds(0, tile_rows)], local_sem.at[0])
    early.start()
    my_rows = pl.ds(pl.multiple_of(f * block, block), block)
    later = pl.ds(tile_rows, rows - tile_rows)
    own = pltpu.make_async_copy(x.at[f], mine.at[:, my_rows, later], local_sem.at[1])
    own.start()
    sends = []
    for i, j in others:
        copy = pltpu.make_async_remote_copy(
            src_ref=x.at[feat_peer(i, j)],
            dst_ref=mine.at[:, my_rows, later],
            send_sem=x_send.at[i * 4 + j],
            recv_sem=x_recv.at[i * 4 + j],
            device_id={"feat": feat_peer(i, j)},
            device_id_type=MESH,
        )
        copy.start()
        sends.append(copy)

    def turn(lo, size):
        def step(i, carry):
            at = pl.multiple_of(i * 128, 128)
            for p in range(2):
                to = pl.multiple_of(p * half_wide + i * 128, 128)
                turned[lo : lo + size, pl.ds(to, 128)] = mine[p, pl.ds(at, 128), lo : lo + size].T
            return carry

        lax.fori_loop(0, half_wide // 128, step, 0)

    def forward(lo, size):
        tile_of = lax.div(lax.broadcasted_iota(jnp.int32, (size, 256), 0) + lo, tile_rows)
        live = tile_of < live_count[0]

        def step(n, carry):
            at = pl.ds(pl.multiple_of(n * 256, 256), 256)
            pre = jnp.dot(turned[lo : lo + size], w[:, at], preferred_element_type=jnp.float32)
            pre = pre + bias[:, at]
            on = live & (pre > 0)
            act[lo : lo + size, at] = jnp.where(on, pre, 0.0).astype(act.dtype)
            c = cot[lo : lo + size, at].astype(jnp.float32)
            delta[lo : lo + size, at] = jnp.where(on, c, 0.0).astype(delta.dtype)
            return carry

        lax.fori_loop(0, hidden // 256, step, 0)

    early.wait()
    turn(0, tile_rows)
    for copy in weights:
        copy.wait()
    forward(0, tile_rows)
    own.wait()
    for copy in sends:
        copy.wait()
    turn(tile_rows, rows - tile_rows)
    forward(tile_rows, rows - tile_rows)

    quarter = cols // 2

    def ours(h):
        return pl.ds(pl.multiple_of(core * cols + h * quarter, quarter), quarter)

    def theirs(h):
        return pl.ds(pl.multiple_of((1 - core) * cols + h * quarter, quarter), quarter)

    def product(p, at):
        return jnp.dot(mine[p], delta[:, at], preferred_element_type=jnp.float32)

    def remote(src, dst, send_sem, recv_sem, peer):
        copy = pltpu.make_async_remote_copy(
            src_ref=src, dst_ref=dst, send_sem=send_sem, recv_sem=recv_sem,
            device_id=peer, device_id_type=MESH,
        )
        copy.start()
        return copy

    def place(h, phase):
        return xx if (h + phase) % 2 == 0 else z

    def neighbour(h, phase, s):
        at = lax.rem(place(h, phase) + 4 + s, 4)
        return {"feat": z * 4 + at if (h + phase) % 2 == 0 else at * 4 + xx}

    phases = ((part_a, relay_a, in_a), (part_b, relay_b, in_b))
    started = {}

    def ring(h, phase, messages):
        part, relay, arrived = (buffer.at[h] for buffer in phases[phase])
        pos = place(h, phase)
        far, after, before = (lax.rem(pos + s, 4) for s in (2, 1, 3))
        plan = (
            (1, part.at[far, 0], relay.at[0]),
            (-1, part.at[far, 1], relay.at[1]),
            (1, part.at[after, 1], arrived.at[0, 1]),
            (-1, part.at[before, 0], arrived.at[1, 0]),
            (1, part.at[after, 0], arrived.at[0, 0]),
            (-1, part.at[before, 1], arrived.at[1, 1]),
        )
        for m in messages:
            step, src, dst = plan[m]
            started[h, phase, m] = remote(
                src, dst, r_send.at[phase, h, m], r_recv.at[phase, h, m], neighbour(h, phase, step)
            )

    def pass_on(h, phase):
        part, relay, _ = (buffer.at[h] for buffer in phases[phase])
        pos = place(h, phase)
        for way, step in ((0, 1), (1, 3)):
            at = lax.rem(pos + step, 4)
            started[h, phase, way].wait_recv()
            part[at, way] = (
                part[at, way].astype(jnp.float32) + relay[way].astype(jnp.float32)
            ).astype(part.dtype)
            ring(h, phase, (4 + way,))

    def gathered(h, phase, p):
        part, _, arrived = (buffer.at[h] for buffer in phases[phase])
        for m in ((4, 3), (2, 5))[p]:
            started[h, phase, m].wait_recv()
        return (
            part[place(h, phase), p].astype(jnp.float32)
            + arrived[0, p].astype(jnp.float32)
            + arrived[1, p].astype(jnp.float32)
        )

    order = ((0, 0), (0, 1), (1, 0), (1, 1))
    pairs = []
    for q, (h, p) in enumerate(order):
        other[q] = product(p, theirs(h)).astype(other.dtype)
        pairs.append(remote(other.at[q], pair_in.at[q], p_send.at[q], p_recv.at[q], partner))
    for q, (h, p) in enumerate(order):
        own_part = product(p, ours(h))
        pairs[q].wait_recv()
        own_part = (own_part + pair_in[q].astype(jnp.float32)).astype(part_a.dtype)
        for i in range(4):
            for j in range(4):
                rows_ij = own_part[(i * 4 + j) * block : (i * 4 + j + 1) * block]
                if h == 0:
                    part_a[h, j, p, i] = rows_ij
                else:
                    part_a[h, i, p, j] = rows_ij
        ring(h, 0, (0, 3) if p == 0 else (1, 2))
        if q >= 2:
            pass_on(q - 2, 0)
    for h in range(2):
        for p in range(2):
            reduced = gathered(h, 0, p).astype(part_b.dtype)
            for i in range(4):
                part_b[h, i, p] = reduced[i]
            ring(h, 1, (0, 3) if p == 0 else (1, 2))
    for h in range(2):
        pass_on(h, 1)

    def y_peer_of(h, stage):
        at = y + 1 - 2 * lax.rem(y, 2) if (h + stage) % 2 == 0 else 3 - y
        return {"dp": at * 2 + core}

    across = {}
    for h in range(2):
        for p in range(2):
            y_out[h, 0, p] = gathered(h, 1, p).astype(y_out.dtype)
        across[h, 0] = remote(
            y_out.at[h, 0], y_in.at[h, 0], y_send.at[h, 0], y_recv.at[h, 0], y_peer_of(h, 0)
        )
    for h in range(2):
        across[h, 0].wait_recv()
        both = y_out[h, 0].astype(jnp.float32) + y_in[h, 0].astype(jnp.float32)
        y_out[h, 1] = both.astype(y_out.dtype)
        across[h, 1] = remote(
            y_out.at[h, 1], y_in.at[h, 1], y_send.at[h, 1], y_recv.at[h, 1], y_peer_of(h, 1)
        )
    last = []
    for h in range(2):
        across[h, 1].wait_recv()
        half[h] = y_out[h, 1].astype(jnp.float32) + y_in[h, 1].astype(jnp.float32)
        last.append(remote(half.at[h], half_in.at[h], h_send.at[h], h_recv.at[h], partner))
        out_self[:, ours(h)] = half[h, 0]
        out_neigh[:, ours(h)] = half[h, 1]
    for h in range(2):
        last[h].wait_recv()
        out_self[:, theirs(h)] = half_in[h, 0]
        out_neigh[:, theirs(h)] = half_in[h, 1]
    for copy in [*pairs, *started.values(), *across.values(), *last]:
        copy.wait_send()


def layer(count, first, x, w_self, w_neigh, bias, cot):
    block, rows = x.shape[2], cot.shape[0]
    half_wide, hidden = w_self.shape
    quarter = hidden // 4
    bf16, f32 = jnp.bfloat16, jnp.float32
    vmem = pl.BlockSpec(memory_space=pltpu.VMEM)
    hbm = pl.BlockSpec(memory_space=pl.ANY)
    dma = pltpu.SemaphoreType.DMA
    return pl.pallas_call(
        layer_kernel,
        in_specs=[pl.BlockSpec(memory_space=pltpu.SMEM), hbm, hbm, hbm, hbm, vmem, vmem],
        out_specs=[vmem, vmem, vmem],
        out_shape=[
            jax.ShapeDtypeStruct((rows, hidden), bf16),
            jax.ShapeDtypeStruct((block, hidden), f32),
            jax.ShapeDtypeStruct((block, hidden), f32),
        ],
        scratch_shapes=[
            pltpu.VMEM((2 * half_wide, hidden), bf16),
            pltpu.VMEM((2, half_wide, rows), bf16),
            pltpu.VMEM((rows, 2 * half_wide), bf16),
            pltpu.VMEM((rows, hidden), bf16),
            pltpu.VMEM((4, half_wide, quarter), bf16),
            pltpu.VMEM((4, half_wide, quarter), bf16),
            pltpu.VMEM((2, 4, 2, 4, block, quarter), bf16),
            pltpu.VMEM((2, 2, 4, block, quarter), bf16),
            pltpu.VMEM((2, 2, 2, 4, block, quarter), bf16),
            pltpu.VMEM((2, 4, 2, block, quarter), bf16),
            pltpu.VMEM((2, 2, block, quarter), bf16),
            pltpu.VMEM((2, 2, 2, block, quarter), bf16),
            pltpu.VMEM((2, 2, 2, block, quarter), bf16),
            pltpu.VMEM((2, 2, 2, block, quarter), bf16),
            pltpu.VMEM((2, 2, block, quarter), f32),
            pltpu.VMEM((2, 2, block, quarter), f32),
            dma((16,)), dma((16,)), dma((4,)), dma((4,)), dma((2, 2, 6)), dma((2, 2, 6)),
            dma((2, 2)), dma((2, 2)), dma((2,)), dma((2,)), dma((2,)), dma((2,)),
        ],
        compiler_params=pltpu.CompilerParams(
            collective_id=0, has_side_effects=True, vmem_limit_bytes=56 << 20
        ),
        cost_estimate=pl.CostEstimate(
            flops=2_500_000_000, bytes_accessed=10_000_000, transcendentals=0
        ),
    )(count, first, x, w_self, w_neigh, bias, cot)


def local(node_table, neighbor_ids, tile_counts, w_self, w_neigh, bias, cotangent):
    owned, rows, hidden = cotangent.shape
    w_self_all = lax.all_gather(w_self, "feat", axis=0, tiled=True)
    w_neigh_all = lax.all_gather(w_neigh, "feat", axis=0, tiled=True)
    ids = neighbor_ids.transpose(1, 0, 2)
    nodes, counts, first = first_tiles(tile_counts, ids, node_table)
    x = gather(counts, ids, nodes, node_table.shape[0])
    act, grad_self, grad_neigh = layer(
        tile_counts,
        first,
        x,
        w_self_all,
        w_neigh_all,
        bias.reshape(1, hidden),
        cotangent.reshape(owned * rows, hidden),
    )
    act, grad_self, grad_neigh = finish(act, grad_self, grad_neigh)
    return act.reshape(owned, rows, hidden), grad_self, grad_neigh


def solution(mesh):
    return jax.shard_map(
        local,
        mesh=mesh,
        in_specs=(
            P("feat", None),
            P("dp", None, None),
            P(("dp", "feat")),
            P("feat", None),
            P("feat", None),
            P(),
            P(("dp", "feat"), None, None),
        ),
        out_specs=(P(("dp", "feat"), None, None), P("feat", None), P("feat", None)),
        check_vma=False,
    )
```

```python
import jax
import jax.numpy as jnp
from jax import lax
from jax.experimental import pallas as pl
from jax.experimental.pallas import tpu as pltpu
from jax.sharding import PartitionSpec as P

MESH = pl.DeviceIdType.MESH
UNROLL = 32
BATCH = 8
CHUNK = 2048
LOADS = 8
DIRECT = (False, True)


def tile_sums(nodes, sums, ids, rows, block, base):
    lane_row = lax.broadcasted_iota(jnp.int32, (1, 128), 1)

    def group(g, carry):
        for u in range(UNROLL):
            r = g * UNROLL + u

            def node(k):
                return nodes[pl.ds(ids[k][base + r], 1), :]

            total = node(1)
            for k in range(2, len(ids)):
                total = total + node(k)
            sums[pl.ds(r, 1), :] = jnp.where(lane_row < block, node(0), total)
        return carry

    lax.fori_loop(0, rows // UNROLL, group, 0)
    held = sums[...]
    lane = lax.broadcasted_iota(jnp.int32, held.shape, 1)
    held = jnp.where(lane < block, held, held / (len(ids) - 1.0))
    return held.T.astype(jnp.bfloat16)


def first_kernel(
    count, ids_hbm, table_hbm, w_self, w_neigh, nodes, counts, first, weights,
    table, sums, sent, landed, got, w_got, *rest
):
    fan, _, rows = ids_hbm.shape
    ids = (rest[:fan], rest[fan : 2 * fan])
    ids_sem, load_sem, c_send, c_recv, x_send, x_recv, w_send, w_recv, w_sem = rest[2 * fan :]
    core = lax.rem(lax.axis_index("dp"), 2)
    block, width = table_hbm.shape
    peers = got.shape[0]
    f = lax.axis_index("feat")
    piece = width // LOADS

    def load(i):
        at = pl.ds(pl.multiple_of(i * piece, piece), piece)
        return pltpu.make_async_copy(table_hbm.at[:, at], table.at[:, at], load_sem.at[i])

    def peer(i):
        return lax.rem(f + i, peers)

    def fetch(i, slot, k):
        return pltpu.make_async_copy(
            ids_hbm.at[k, peer(i) * 3], ids[slot][k], ids_sem.at[slot, k]
        )

    for i in range(LOADS):
        load(i).start()
    for k in range(fan):
        fetch(1, 0, k).start()
    barrier = pltpu.get_barrier_semaphore()
    for i in range(1, peers):
        pl.semaphore_signal(barrier, inc=1, device_id={"feat": peer(i)}, device_id_type=MESH)
    got[f] = jnp.zeros(got.shape[1:], jnp.int32) + count[0]

    def fill(i, carry):
        load(i).wait()

        def turn(j, inner):
            at = pl.multiple_of(i * piece + j * CHUNK, CHUNK)
            part = table[:, pl.ds(at, CHUNK)]
            wide = jnp.concatenate([part, part, jnp.zeros((128 - 2 * block, CHUNK), part.dtype)], 0)
            nodes[pl.ds(at, CHUNK), :] = wide.T.astype(jnp.float32)
            return inner

        lax.fori_loop(0, piece // CHUNK, turn, 0)
        return carry

    lax.fori_loop(0, LOADS, fill, 0)
    pl.semaphore_wait(barrier, peers - 1)

    def count_copy(i):
        return pltpu.make_async_remote_copy(
            src_ref=got.at[f], dst_ref=got.at[f], send_sem=c_send.at[i], recv_sem=c_recv.at[i],
            device_id={"feat": peer(i)}, device_id_type=MESH,
        )

    my_rows = pl.ds(pl.multiple_of(f * block, block), block)

    def weight_copy(source, i):
        return pltpu.make_async_remote_copy(
            src_ref=source, dst_ref=w_got.at[my_rows], send_sem=w_send.at[i], recv_sem=w_recv.at[i],
            device_id={"feat": peer(i)}, device_id_type=MESH,
        )

    def tile_copy(i):
        return pltpu.make_async_remote_copy(
            src_ref=sent.at[peer(i)], dst_ref=landed.at[:, my_rows],
            send_sem=x_send.at[i], recv_sem=x_recv.at[i],
            device_id={"feat": peer(i)}, device_id_type=MESH,
        )

    for i in range(1, peers):
        count_copy(i).start()
    for which, source in enumerate((w_self, w_neigh)):

        @pl.when(core == which)
        def _():
            keep = pltpu.make_async_copy(source, w_got.at[my_rows], w_sem)
            keep.start()
            for i in range(1, peers):
                weight_copy(source, i).start()
            keep.wait()

    def pair(p, carry):
        for slot in range(2):
            i = p * 2 + slot + 1
            for k in range(fan):
                fetch(i, slot, k).wait()
            if slot == 0:
                for k in range(fan):
                    fetch(i + 1, 1, k).start()
            else:

                @pl.when(i < peers)
                def _():
                    for k in range(fan):
                        fetch(i + 1, 0, k).start()

            turned = tile_sums(nodes, sums, ids[slot], rows, block, 0)
            for part in range(2):
                sent[peer(i), part] = turned[part * block : (part + 1) * block]

            @pl.when(i < peers)
            def _():
                tile_copy(i).start()

        return carry

    lax.fori_loop(0, peers // 2, pair, 0)
    for part in range(2):
        landed[part, my_rows] = sent[f, part]

    def settle(i, carry):
        count_copy(i).wait()
        tile_copy(i).wait()
        weight_copy(w_self, i).wait()
        return carry

    lax.fori_loop(1, peers, settle, 0)
    keep = pltpu.make_async_copy(w_got, weights, w_sem)
    keep.start()
    keep.wait()
    counts[...] = got[...]
    first[...] = landed[...]


def first_tiles(count, ids, table, w_self, w_neigh):
    fan, tiles, rows = ids.shape
    block, width = table.shape
    hidden = w_self.shape[1]
    peers = tiles // 3
    dma = pltpu.SemaphoreType.DMA
    hbm = pl.BlockSpec(memory_space=pl.ANY)
    vmem = pl.BlockSpec(memory_space=pltpu.VMEM)
    nodes, counts, first, weights = pl.pallas_call(
        first_kernel,
        in_specs=[pl.BlockSpec(memory_space=pltpu.SMEM), hbm, hbm, hbm, hbm],
        out_specs=[vmem, vmem, vmem, hbm],
        out_shape=[
            pltpu.VMEM((width, 128), jnp.float32),
            jax.ShapeDtypeStruct((peers, 1, 128), jnp.int32),
            jax.ShapeDtypeStruct((2, peers * block, rows), jnp.bfloat16),
            jax.ShapeDtypeStruct((peers * block, hidden), w_self.dtype),
        ],
        scratch_shapes=[
            pltpu.VMEM((block, width), table.dtype),
            pltpu.VMEM((rows, 128), jnp.float32),
            pltpu.VMEM((peers, 2, block, rows), jnp.bfloat16),
            pltpu.VMEM((2, peers * block, rows), jnp.bfloat16),
            pltpu.VMEM((peers, 1, 128), jnp.int32),
            pltpu.VMEM((peers * block, hidden), w_self.dtype),
        ]
        + [pltpu.SMEM((rows,), jnp.int32)] * (2 * fan)
        + [dma((2, fan)), dma((LOADS,))]
        + [dma((peers,))] * 6
        + [dma],
        compiler_params=pltpu.CompilerParams(
            collective_id=1, has_side_effects=True, vmem_limit_bytes=28 << 20
        ),
        cost_estimate=pl.CostEstimate(
            flops=60_000_000_000, bytes_accessed=150_000_000, transcendentals=0
        ),
    )(count, ids, table, w_self, w_neigh)
    return pltpu.with_memory_space_constraint(nodes, pltpu.VMEM), counts, first, weights


def gather_kernel(counts, ids_hbm, nodes, out, sums, *rest):
    fan, tiles, rows = ids_hbm.shape
    ids, sem = (rest[:fan], rest[fan : 2 * fan]), rest[2 * fan]
    block = out.shape[2]
    flat = [[ref.reshape(BATCH * rows) for ref in refs] for refs in ids]

    def fetch(batch, slot, k):
        return pltpu.make_async_copy(
            ids_hbm.at[k, pl.ds(batch * BATCH, BATCH)], ids[slot][k], sem.at[slot, k]
        )

    for k in range(fan):
        fetch(0, 0, k).start()

    def one_batch(batch, slot):
        def tile(j, carry):
            t = batch * BATCH + j
            m, place = lax.div(t, 3), lax.rem(t, 3)
            live = place < counts[m, 0, 0]
            at = pl.ds(pl.multiple_of(jnp.maximum(place - 1, 0) * rows, rows), rows)

            @pl.when(live & (place > 0))
            def _():
                turned = tile_sums(nodes, sums, flat[slot], rows, block, j * rows)
                out[m, 0, :, at] = turned[:block]
                out[m, 1, :, at] = turned[block : 2 * block]

            @pl.when(jnp.logical_not(live))
            def _():
                out[m, :, :, at] = jnp.zeros((2, block, rows), out.dtype)

            return carry

        lax.fori_loop(0, BATCH, tile, 0)

    batches = tiles // BATCH

    def pair(p, carry):
        for slot in range(2):
            batch = p * 2 + slot
            for k in range(fan):
                fetch(batch, slot, k).wait()
            if slot == 0:
                for k in range(fan):
                    fetch(batch + 1, 1, k).start()
            else:

                @pl.when(batch < batches - 1)
                def _():
                    for k in range(fan):
                        fetch(batch + 1, 0, k).start()

            one_batch(batch, slot)
        return carry

    lax.fori_loop(0, batches // 2, pair, 0)


def gather(counts, ids, nodes, block):
    fan, tiles, rows = ids.shape
    vmem = pl.BlockSpec(memory_space=pltpu.VMEM)
    return pl.pallas_call(
        gather_kernel,
        in_specs=[pl.BlockSpec(memory_space=pltpu.SMEM), pl.BlockSpec(memory_space=pl.ANY), vmem],
        out_specs=vmem,
        scratch_shapes=[pltpu.VMEM((rows, 128), jnp.float32)]
        + [pltpu.SMEM((BATCH, rows), jnp.int32)] * (2 * fan)
        + [pltpu.SemaphoreType.DMA((2, fan))],
        out_shape=jax.ShapeDtypeStruct((tiles // 3, 2, block, 2 * rows), jnp.bfloat16),
        compiler_params=pltpu.CompilerParams(vmem_limit_bytes=28 << 20),
        cost_estimate=pl.CostEstimate(
            flops=60_000_000_000, bytes_accessed=150_000_000, transcendentals=0
        ),
    )(counts, ids, nodes)


def finish_kernel(a, b, c, out_a, out_b, out_c, held_a, held_b, held_c, sem):
    moves = []
    for q in range(4):
        at = pl.ds(q * (a.shape[0] // 4), a.shape[0] // 4)
        moves.append((a.at[at], held_a.at[at], out_a.at[at]))
    moves += [(b, held_b, out_b), (c, held_c, out_c)]
    ins = [pltpu.make_async_copy(x, h, sem.at[0, i]) for i, (x, h, _) in enumerate(moves)]
    outs = [pltpu.make_async_copy(h, o, sem.at[1, i]) for i, (_, h, o) in enumerate(moves)]
    for copy in ins:
        copy.start()
    for arrived, leaving in zip(ins, outs):
        arrived.wait()
        leaving.start()
    for copy in outs:
        copy.wait()


def finish(*arrays):
    return pl.pallas_call(
        finish_kernel,
        in_specs=[pl.BlockSpec(memory_space=pl.ANY)] * 3,
        out_specs=[pl.BlockSpec(memory_space=pl.ANY)] * 3,
        out_shape=[jax.ShapeDtypeStruct(x.shape, x.dtype) for x in arrays],
        scratch_shapes=[pltpu.VMEM(x.shape, x.dtype) for x in arrays]
        + [pltpu.SemaphoreType.DMA((2, 6))],
        compiler_params=pltpu.CompilerParams(vmem_limit_bytes=56 << 20),
    )(*arrays)


def layer_kernel(
    live_count, first, x, w_half, bias, cot, act, out_self, out_neigh,
    w, mine, turned, delta, other, pair_in, part_a, relay_a, in_a, part_b, relay_b, in_b,
    y_in, half, half_in, x_send, x_recv, p_send, p_recv, r_send, r_recv, y_send, y_recv, h_send, h_recv, local_sem, w_sem,
):
    f, d = lax.axis_index("feat"), lax.axis_index("dp")
    z, xx = lax.div(f, 4), lax.rem(f, 4)
    y, core = lax.div(d, 2), lax.rem(d, 2)
    partner = {"dp": y * 2 + (1 - core)}
    half_wide, rows = mine.shape[1:]
    block = x.shape[2]
    hidden = w.shape[1]
    cols = hidden // 2

    def feat_peer(i, j):
        return lax.rem(z + i, 4) * 4 + lax.rem(xx + j, 4)

    def y_peer(i):
        return {"dp": lax.rem(y + i, 4) * 2 + core}

    others = [(i, j) for i in range(4) for j in range(4) if (i, j) != (0, 0)]

    w_rows = pl.ds(pl.multiple_of(core * half_wide, half_wide), half_wide)
    w_own = pltpu.make_async_copy(w_half, w.at[w_rows], w_sem.at[0])
    w_own.start()

    barrier = pltpu.get_barrier_semaphore()
    for i, j in others:
        pl.semaphore_signal(barrier, inc=1, device_id={"feat": feat_peer(i, j)}, device_id_type=MESH)
    pl.semaphore_signal(barrier, inc=1, device_id=partner, device_id_type=MESH)
    for i in range(1, 4):
        pl.semaphore_signal(barrier, inc=1, device_id=y_peer(i), device_id_type=MESH)
    pl.semaphore_wait(barrier, 19)

    w_other = pltpu.make_async_remote_copy(
        src_ref=w_half, dst_ref=w.at[w_rows], send_sem=w_sem.at[1], recv_sem=w_sem.at[2],
        device_id=partner, device_id_type=MESH,
    )
    w_other.start()
    tile_rows = rows // 3
    early = pltpu.make_async_copy(first, mine.at[:, :, pl.ds(0, tile_rows)], local_sem.at[0])
    early.start()
    my_rows = pl.ds(pl.multiple_of(f * block, block), block)
    later = pl.ds(tile_rows, rows - tile_rows)
    own = pltpu.make_async_copy(x.at[f], mine.at[:, my_rows, later], local_sem.at[1])
    own.start()
    sends = []
    for i, j in others:
        copy = pltpu.make_async_remote_copy(
            src_ref=x.at[feat_peer(i, j)],
            dst_ref=mine.at[:, my_rows, later],
            send_sem=x_send.at[i * 4 + j],
            recv_sem=x_recv.at[i * 4 + j],
            device_id={"feat": feat_peer(i, j)},
            device_id_type=MESH,
        )
        copy.start()
        sends.append(copy)

    def turn(lo, size):
        def step(i, carry):
            at = pl.multiple_of(i * 128, 128)
            for p in range(2):
                to = pl.multiple_of(p * half_wide + i * 128, 128)
                turned[lo : lo + size, pl.ds(to, 128)] = mine[p, pl.ds(at, 128), lo : lo + size].T
            return carry

        lax.fori_loop(0, half_wide // 128, step, 0)

    def forward(lo, size):
        tile_of = lax.div(lax.broadcasted_iota(jnp.int32, (size, 256), 0) + lo, tile_rows)
        live = tile_of < live_count[0]

        def step(n, carry):
            at = pl.ds(pl.multiple_of(n * 256, 256), 256)
            pre = jnp.dot(turned[lo : lo + size], w[:, at], preferred_element_type=jnp.float32)
            pre = pre + bias[:, at]
            on = live & (pre > 0)
            act[lo : lo + size, at] = jnp.where(on, pre, 0.0).astype(act.dtype)
            c = cot[lo : lo + size, at].astype(jnp.float32)
            delta[lo : lo + size, at] = jnp.where(on, c, 0.0).astype(delta.dtype)
            return carry

        lax.fori_loop(0, hidden // 256, step, 0)

    early.wait()
    turn(0, tile_rows)
    w_own.wait()
    w_other.wait()
    forward(0, tile_rows)
    own.wait()
    for copy in sends:
        copy.wait()
    turn(tile_rows, rows - tile_rows)
    forward(tile_rows, rows - tile_rows)

    quarter = cols // 2

    def ours(h):
        return pl.ds(pl.multiple_of(core * cols + h * quarter, quarter), quarter)

    def theirs(h):
        return pl.ds(pl.multiple_of((1 - core) * cols + h * quarter, quarter), quarter)

    def product(p, at):
        return jnp.dot(mine[p], delta[:, at], preferred_element_type=jnp.float32)

    def remote(src, dst, send_sem, recv_sem, peer):
        copy = pltpu.make_async_remote_copy(
            src_ref=src, dst_ref=dst, send_sem=send_sem, recv_sem=recv_sem,
            device_id=peer, device_id_type=MESH,
        )
        copy.start()
        return copy

    def place(h, phase):
        return xx if (h + phase) % 2 == 0 else z

    def neighbour(h, phase, s):
        at = lax.rem(place(h, phase) + 4 + s, 4)
        return {"feat": z * 4 + at if (h + phase) % 2 == 0 else at * 4 + xx}

    phases = ((part_a, relay_a, in_a), (part_b, relay_b, in_b))
    started = {}

    def ring(h, phase, messages):
        part, relay, arrived = (buffer.at[h] for buffer in phases[phase])
        pos = place(h, phase)
        far, after, before = (lax.rem(pos + s, 4) for s in (2, 1, 3))
        plan = (
            (1, part.at[far, 0], relay.at[0]),
            (-1, part.at[far, 1], relay.at[1]),
            (1, part.at[after, 1], arrived.at[0, 1]),
            (-1, part.at[before, 0], arrived.at[1, 0]),
            (1, part.at[after, 0], arrived.at[0, 0]),
            (-1, part.at[before, 1], arrived.at[1, 1]),
        )
        for m in messages:
            step, src, dst = plan[m]
            started[h, phase, m] = remote(
                src, dst, r_send.at[phase, h, m], r_recv.at[phase, h, m], neighbour(h, phase, step)
            )

    def direct(h, phase, p):
        part, _, arrived = (buffer.at[h] for buffer in phases[phase])
        for s in (2, 1, 3):
            m = (s - 1) * 2 + p
            started[h, phase, m] = remote(
                part.at[lax.rem(place(h, phase) + s, 4), p], arrived.at[s - 1, p],
                r_send.at[phase, h, m], r_recv.at[phase, h, m], neighbour(h, phase, s),
            )

    def send_part(h, phase, p):
        if DIRECT[phase]:
            direct(h, phase, p)
        else:
            ring(h, phase, (0, 3) if p == 0 else (1, 2))

    def pass_on(h, phase):
        if DIRECT[phase]:
            return
        part, relay, _ = (buffer.at[h] for buffer in phases[phase])
        pos = place(h, phase)
        for way, step in ((0, 1), (1, 3)):
            at = lax.rem(pos + step, 4)
            started[h, phase, way].wait_recv()
            part[at, way] = (
                part[at, way].astype(jnp.float32) + relay[way].astype(jnp.float32)
            ).astype(part.dtype)
            ring(h, phase, (4 + way,))

    def gathered(h, phase, p):
        part, _, arrived = (buffer.at[h] for buffer in phases[phase])
        from_peers = (p, 2 + p, 4 + p) if DIRECT[phase] else ((4, 3), (2, 5))[p]
        total = part[place(h, phase), p].astype(jnp.float32)
        for m in from_peers:
            started[h, phase, m].wait_recv()
        for i in range(len(from_peers)):
            total = total + arrived[i, p].astype(jnp.float32)
        return total

    order = ((0, 0), (0, 1), (1, 0), (1, 1))
    pairs = []
    for q, (h, p) in enumerate(order):
        other[q] = product(p, theirs(h)).astype(other.dtype)
        pairs.append(remote(other.at[q], pair_in.at[q], p_send.at[q], p_recv.at[q], partner))
    for q, (h, p) in enumerate(order):
        own_part = product(p, ours(h))
        pairs[q].wait_recv()
        own_part = (own_part + pair_in[q].astype(jnp.float32)).astype(part_a.dtype)
        for i in range(4):
            for j in range(4):
                rows_ij = own_part[(i * 4 + j) * block : (i * 4 + j + 1) * block]
                if h == 0:
                    part_a[h, j, p, i] = rows_ij
                else:
                    part_a[h, i, p, j] = rows_ij
        send_part(h, 0, p)
        if q >= 2:
            pass_on(q - 2, 0)
    for h in range(2):
        for p in range(2):
            reduced = gathered(h, 0, p).astype(part_b.dtype)
            for i in range(4):
                part_b[h, i, p] = reduced[i]
            send_part(h, 1, p)
    for h in range(2):
        pass_on(h, 1)

    across = {}
    for h in range(2):
        for p in range(2):
            y_in[h, y, p] = gathered(h, 1, p).astype(y_in.dtype)
        for i in (2, 1, 3):
            across[h, i] = remote(
                y_in.at[h, y], y_in.at[h, y], y_send.at[h, i], y_recv.at[h, i], y_peer(i)
            )
    last = []
    for h in range(2):
        for i in range(1, 4):
            across[h, i].wait_recv()
        total = y_in[h, 0].astype(jnp.float32)
        for i in range(1, 4):
            total = total + y_in[h, i].astype(jnp.float32)
        half[h] = total
        last.append(remote(half.at[h], half_in.at[h], h_send.at[h], h_recv.at[h], partner))
        out_self[:, ours(h)] = half[h, 0]
        out_neigh[:, ours(h)] = half[h, 1]
    for h in range(2):
        last[h].wait_recv()
        out_self[:, theirs(h)] = half_in[h, 0]
        out_neigh[:, theirs(h)] = half_in[h, 1]
    for copy in [*pairs, *started.values(), *across.values(), *last]:
        copy.wait_send()


def layer(count, first, x, w_half, bias, cot):
    block, rows = x.shape[2], cot.shape[0]
    half_wide, hidden = w_half.shape
    quarter = hidden // 4
    bf16, f32 = jnp.bfloat16, jnp.float32
    vmem = pl.BlockSpec(memory_space=pltpu.VMEM)
    hbm = pl.BlockSpec(memory_space=pl.ANY)
    dma = pltpu.SemaphoreType.DMA
    return pl.pallas_call(
        layer_kernel,
        in_specs=[pl.BlockSpec(memory_space=pltpu.SMEM), hbm, hbm, hbm, vmem, vmem],
        out_specs=[vmem, vmem, vmem],
        out_shape=[
            jax.ShapeDtypeStruct((rows, hidden), bf16),
            jax.ShapeDtypeStruct((block, hidden), f32),
            jax.ShapeDtypeStruct((block, hidden), f32),
        ],
        scratch_shapes=[
            pltpu.VMEM((2 * half_wide, hidden), bf16),
            pltpu.VMEM((2, half_wide, rows), bf16),
            pltpu.VMEM((rows, 2 * half_wide), bf16),
            pltpu.VMEM((rows, hidden), bf16),
            pltpu.VMEM((4, half_wide, quarter), bf16),
            pltpu.VMEM((4, half_wide, quarter), bf16),
            pltpu.VMEM((2, 4, 2, 4, block, quarter), bf16),
            pltpu.VMEM((2, 2, 4, block, quarter), bf16),
            pltpu.VMEM((2, 3, 2, 4, block, quarter), bf16),
            pltpu.VMEM((2, 4, 2, block, quarter), bf16),
            pltpu.VMEM((2, 2, block, quarter), bf16),
            pltpu.VMEM((2, 3, 2, block, quarter), bf16),
            pltpu.VMEM((2, 4, 2, block, quarter), bf16),
            pltpu.VMEM((2, 2, block, quarter), f32),
            pltpu.VMEM((2, 2, block, quarter), f32),
            dma((16,)), dma((16,)), dma((4,)), dma((4,)), dma((2, 2, 6)), dma((2, 2, 6)),
            dma((2, 4)), dma((2, 4)), dma((2,)), dma((2,)), dma((2,)), dma((3,)),
        ],
        compiler_params=pltpu.CompilerParams(
            collective_id=0, has_side_effects=True, vmem_limit_bytes=56 << 20
        ),
        cost_estimate=pl.CostEstimate(
            flops=2_500_000_000, bytes_accessed=10_000_000, transcendentals=0
        ),
    )(count, first, x, w_half, bias, cot)


def local(node_table, neighbor_ids, tile_counts, w_self, w_neigh, bias, cotangent):
    owned, rows, hidden = cotangent.shape
    ids = neighbor_ids.transpose(1, 0, 2)
    nodes, counts, first, w_half = first_tiles(tile_counts, ids, node_table, w_self, w_neigh)
    x = gather(counts, ids, nodes, node_table.shape[0])
    act, grad_self, grad_neigh = layer(
        tile_counts,
        first,
        x,
        w_half,
        bias.reshape(1, hidden),
        cotangent.reshape(owned * rows, hidden),
    )
    act, grad_self, grad_neigh = finish(act, grad_self, grad_neigh)
    return act.reshape(owned, rows, hidden), grad_self, grad_neigh


def solution(mesh):
    return jax.shard_map(
        local,
        mesh=mesh,
        in_specs=(
            P("feat", None),
            P("dp", None, None),
            P(("dp", "feat")),
            P("feat", None),
            P("feat", None),
            P(),
            P(("dp", "feat"), None, None),
        ),
        out_specs=(P(("dp", "feat"), None, None), P("feat", None), P("feat", None)),
        check_vma=False,
    )
```

```python
import jax
import jax.numpy as jnp
from jax import lax
from jax.experimental import pallas as pl
from jax.experimental.pallas import tpu as pltpu
from jax.sharding import PartitionSpec as P

MESH = pl.DeviceIdType.MESH
UNROLL = 32
BATCH = 8
CHUNK = 4096
LOADS = 8


def tile_sums(nodes, sums, ids, rows, block, base):
    lane_row = lax.broadcasted_iota(jnp.int32, (1, 128), 1)

    def group(g, carry):
        for u in range(UNROLL):
            r = g * UNROLL + u

            def node(k):
                return nodes[pl.ds(ids[k][base + r], 1), :]

            total = node(1)
            for k in range(2, len(ids)):
                total = total + node(k)
            sums[pl.ds(r, 1), :] = jnp.where(lane_row < block, node(0), total)
        return carry

    lax.fori_loop(0, rows // UNROLL, group, 0)
    held = sums[...]
    lane = lax.broadcasted_iota(jnp.int32, held.shape, 1)
    held = jnp.where(lane < block, held, held / (len(ids) - 1.0))
    return held.T.astype(jnp.bfloat16)


def first_kernel(
    count, ids_hbm, table_hbm, w_self, w_neigh, nodes, counts, first, weights,
    table, sums, sent, landed, got, w_got, *rest
):
    fan, _, rows = ids_hbm.shape
    ids = (rest[:fan], rest[fan : 2 * fan])
    ids_sem, load_sem, c_send, c_recv, x_send, x_recv, w_send, w_recv, w_sem = rest[2 * fan :]
    core = lax.rem(lax.axis_index("dp"), 2)
    block, width = table_hbm.shape
    peers = got.shape[0]
    f = lax.axis_index("feat")
    piece = width // LOADS

    def load(i):
        at = pl.ds(pl.multiple_of(i * piece, piece), piece)
        return pltpu.make_async_copy(table_hbm.at[:, at], table.at[:, at], load_sem.at[i])

    def peer(i):
        return lax.rem(f + i, peers)

    def fetch(i, slot, k):
        return pltpu.make_async_copy(
            ids_hbm.at[k, peer(i) * 3], ids[slot][k], ids_sem.at[slot, k]
        )

    for i in range(LOADS):
        load(i).start()
    for k in range(fan):
        fetch(1, 0, k).start()
    barrier = pltpu.get_barrier_semaphore()
    for i in range(1, peers):
        pl.semaphore_signal(barrier, inc=1, device_id={"feat": peer(i)}, device_id_type=MESH)
    got[f] = jnp.zeros(got.shape[1:], jnp.int32) + count[0]

    def fill(i, carry):
        load(i).wait()

        def turn(j, inner):
            at = pl.multiple_of(i * piece + j * CHUNK, CHUNK)
            part = table[:, pl.ds(at, CHUNK)]
            wide = jnp.concatenate([part, part, jnp.zeros((128 - 2 * block, CHUNK), part.dtype)], 0)
            nodes[pl.ds(at, CHUNK), :] = wide.T.astype(jnp.float32)
            return inner

        lax.fori_loop(0, piece // CHUNK, turn, 0)
        return carry

    lax.fori_loop(0, 2, fill, 0)
    pl.semaphore_wait(barrier, peers - 1)

    def count_copy(i):
        return pltpu.make_async_remote_copy(
            src_ref=got.at[f], dst_ref=got.at[f], send_sem=c_send.at[i], recv_sem=c_recv.at[i],
            device_id={"feat": peer(i)}, device_id_type=MESH,
        )

    my_rows = pl.ds(pl.multiple_of(f * block, block), block)

    def weight_copy(source, i):
        return pltpu.make_async_remote_copy(
            src_ref=source, dst_ref=w_got.at[my_rows], send_sem=w_send.at[i], recv_sem=w_recv.at[i],
            device_id={"feat": peer(i)}, device_id_type=MESH,
        )

    def tile_copy(i):
        return pltpu.make_async_remote_copy(
            src_ref=sent.at[peer(i)], dst_ref=landed.at[:, my_rows],
            send_sem=x_send.at[i], recv_sem=x_recv.at[i],
            device_id={"feat": peer(i)}, device_id_type=MESH,
        )

    for i in range(1, peers):
        count_copy(i).start()
    for which, source in enumerate((w_self, w_neigh)):

        @pl.when(core == which)
        def _():
            keep = pltpu.make_async_copy(source, w_got.at[my_rows], w_sem)
            keep.start()
            for i in range(1, peers):
                weight_copy(source, i).start()
            keep.wait()

    lax.fori_loop(2, LOADS, fill, 0)

    def pair(p, carry):
        for slot in range(2):
            i = p * 2 + slot + 1
            for k in range(fan):
                fetch(i, slot, k).wait()
            if slot == 0:
                for k in range(fan):
                    fetch(i + 1, 1, k).start()
            else:

                @pl.when(i < peers)
                def _():
                    for k in range(fan):
                        fetch(i + 1, 0, k).start()

            turned = tile_sums(nodes, sums, ids[slot], rows, block, 0)
            for part in range(2):
                sent[peer(i), part] = turned[part * block : (part + 1) * block]

            @pl.when(i < peers)
            def _():
                tile_copy(i).start()

        return carry

    lax.fori_loop(0, peers // 2, pair, 0)
    for part in range(2):
        landed[part, my_rows] = sent[f, part]

    def settle(i, carry):
        count_copy(i).wait()
        tile_copy(i).wait()
        weight_copy(w_self, i).wait()
        return carry

    lax.fori_loop(1, peers, settle, 0)
    keep = pltpu.make_async_copy(w_got, weights, w_sem)
    keep.start()
    keep.wait()
    counts[...] = got[...]
    first[...] = landed[...]


def first_tiles(count, ids, table, w_self, w_neigh):
    fan, tiles, rows = ids.shape
    block, width = table.shape
    hidden = w_self.shape[1]
    peers = tiles // 3
    dma = pltpu.SemaphoreType.DMA
    hbm = pl.BlockSpec(memory_space=pl.ANY)
    vmem = pl.BlockSpec(memory_space=pltpu.VMEM)
    nodes, counts, first, weights = pl.pallas_call(
        first_kernel,
        in_specs=[pl.BlockSpec(memory_space=pltpu.SMEM), hbm, hbm, hbm, hbm],
        out_specs=[vmem, vmem, vmem, hbm],
        out_shape=[
            pltpu.VMEM((width, 128), jnp.float32),
            jax.ShapeDtypeStruct((peers, 1, 128), jnp.int32),
            jax.ShapeDtypeStruct((2, peers * block, rows), jnp.bfloat16),
            jax.ShapeDtypeStruct((peers * block, hidden), w_self.dtype),
        ],
        scratch_shapes=[
            pltpu.VMEM((block, width), table.dtype),
            pltpu.VMEM((rows, 128), jnp.float32),
            pltpu.VMEM((peers, 2, block, rows), jnp.bfloat16),
            pltpu.VMEM((2, peers * block, rows), jnp.bfloat16),
            pltpu.VMEM((peers, 1, 128), jnp.int32),
            pltpu.VMEM((peers * block, hidden), w_self.dtype),
        ]
        + [pltpu.SMEM((rows,), jnp.int32)] * (2 * fan)
        + [dma((2, fan)), dma((LOADS,))]
        + [dma((peers,))] * 6
        + [dma],
        compiler_params=pltpu.CompilerParams(
            collective_id=1, has_side_effects=True, vmem_limit_bytes=28 << 20
        ),
        cost_estimate=pl.CostEstimate(
            flops=60_000_000_000, bytes_accessed=150_000_000, transcendentals=0
        ),
    )(count, ids, table, w_self, w_neigh)
    return pltpu.with_memory_space_constraint(nodes, pltpu.VMEM), counts, first, weights


def gather_kernel(counts, ids_hbm, nodes, out, sums, *rest):
    fan, tiles, rows = ids_hbm.shape
    ids, sem = (rest[:fan], rest[fan : 2 * fan]), rest[2 * fan]
    block = out.shape[2]
    flat = [[ref.reshape(BATCH * rows) for ref in refs] for refs in ids]

    def fetch(batch, slot, k):
        return pltpu.make_async_copy(
            ids_hbm.at[k, pl.ds(batch * BATCH, BATCH)], ids[slot][k], sem.at[slot, k]
        )

    for k in range(fan):
        fetch(0, 0, k).start()

    def one_batch(batch, slot):
        def tile(j, carry):
            t = batch * BATCH + j
            m, place = lax.div(t, 3), lax.rem(t, 3)
            live = place < counts[m, 0, 0]
            at = pl.ds(pl.multiple_of(jnp.maximum(place - 1, 0) * rows, rows), rows)

            @pl.when(live & (place > 0))
            def _():
                turned = tile_sums(nodes, sums, flat[slot], rows, block, j * rows)
                out[m, 0, :, at] = turned[:block]
                out[m, 1, :, at] = turned[block : 2 * block]

            @pl.when(jnp.logical_not(live))
            def _():
                out[m, :, :, at] = jnp.zeros((2, block, rows), out.dtype)

            return carry

        lax.fori_loop(0, BATCH, tile, 0)

    batches = tiles // BATCH

    def pair(p, carry):
        for slot in range(2):
            batch = p * 2 + slot
            for k in range(fan):
                fetch(batch, slot, k).wait()
            if slot == 0:
                for k in range(fan):
                    fetch(batch + 1, 1, k).start()
            else:

                @pl.when(batch < batches - 1)
                def _():
                    for k in range(fan):
                        fetch(batch + 1, 0, k).start()

            one_batch(batch, slot)
        return carry

    lax.fori_loop(0, batches // 2, pair, 0)


def gather(counts, ids, nodes, block):
    fan, tiles, rows = ids.shape
    vmem = pl.BlockSpec(memory_space=pltpu.VMEM)
    return pl.pallas_call(
        gather_kernel,
        in_specs=[pl.BlockSpec(memory_space=pltpu.SMEM), pl.BlockSpec(memory_space=pl.ANY), vmem],
        out_specs=vmem,
        scratch_shapes=[pltpu.VMEM((rows, 128), jnp.float32)]
        + [pltpu.SMEM((BATCH, rows), jnp.int32)] * (2 * fan)
        + [pltpu.SemaphoreType.DMA((2, fan))],
        out_shape=jax.ShapeDtypeStruct((tiles // 3, 2, block, 2 * rows), jnp.bfloat16),
        compiler_params=pltpu.CompilerParams(vmem_limit_bytes=28 << 20),
        cost_estimate=pl.CostEstimate(
            flops=60_000_000_000, bytes_accessed=150_000_000, transcendentals=0
        ),
    )(counts, ids, nodes)


def finish_kernel(a, b, c, out_a, out_b, out_c, held_a, held_b, held_c, sem):
    moves = []
    for q in range(4):
        at = pl.ds(q * (a.shape[0] // 4), a.shape[0] // 4)
        moves.append((a.at[at], held_a.at[at], out_a.at[at]))
    moves += [(b, held_b, out_b), (c, held_c, out_c)]
    ins = [pltpu.make_async_copy(x, h, sem.at[0, i]) for i, (x, h, _) in enumerate(moves)]
    outs = [pltpu.make_async_copy(h, o, sem.at[1, i]) for i, (_, h, o) in enumerate(moves)]
    for copy in ins:
        copy.start()
    for arrived, leaving in zip(ins, outs):
        arrived.wait()
        leaving.start()
    for copy in outs:
        copy.wait()


def finish(*arrays):
    return pl.pallas_call(
        finish_kernel,
        in_specs=[pl.BlockSpec(memory_space=pl.ANY)] * 3,
        out_specs=[pl.BlockSpec(memory_space=pl.ANY)] * 3,
        out_shape=[jax.ShapeDtypeStruct(x.shape, x.dtype) for x in arrays],
        scratch_shapes=[pltpu.VMEM(x.shape, x.dtype) for x in arrays]
        + [pltpu.SemaphoreType.DMA((2, 6))],
        compiler_params=pltpu.CompilerParams(vmem_limit_bytes=56 << 20),
    )(*arrays)


def layer_kernel(
    live_count, first, x, w_half, bias, cot, act, out_self, out_neigh,
    w, mine, turned, delta, other, pair_in, part_a, in_a, part_b, in_b,
    y_in, half, half_in, x_send, x_recv, p_send, p_recv, r_send, r_recv, y_send, y_recv, h_send, h_recv, local_sem, w_sem,
):
    f, d = lax.axis_index("feat"), lax.axis_index("dp")
    z, xx = lax.div(f, 4), lax.rem(f, 4)
    y, core = lax.div(d, 2), lax.rem(d, 2)
    partner = {"dp": y * 2 + (1 - core)}
    half_wide, rows = mine.shape[1:]
    block = x.shape[2]
    hidden = w.shape[1]
    cols = hidden // 2

    def feat_peer(i, j):
        return lax.rem(z + i, 4) * 4 + lax.rem(xx + j, 4)

    def y_peer(i):
        return {"dp": lax.rem(y + i, 4) * 2 + core}

    others = [(i, j) for i in range(4) for j in range(4) if (i, j) != (0, 0)]

    w_rows = pl.ds(pl.multiple_of(core * half_wide, half_wide), half_wide)
    w_own = pltpu.make_async_copy(w_half, w.at[w_rows], w_sem.at[0])
    w_own.start()

    barrier = pltpu.get_barrier_semaphore()
    for i, j in others:
        pl.semaphore_signal(barrier, inc=1, device_id={"feat": feat_peer(i, j)}, device_id_type=MESH)
    pl.semaphore_signal(barrier, inc=1, device_id=partner, device_id_type=MESH)
    for i in range(1, 4):
        pl.semaphore_signal(barrier, inc=1, device_id=y_peer(i), device_id_type=MESH)
    pl.semaphore_wait(barrier, 19)

    w_other = pltpu.make_async_remote_copy(
        src_ref=w_half, dst_ref=w.at[w_rows], send_sem=w_sem.at[1], recv_sem=w_sem.at[2],
        device_id=partner, device_id_type=MESH,
    )
    w_other.start()
    tile_rows = rows // 3
    early = pltpu.make_async_copy(first, mine.at[:, :, pl.ds(0, tile_rows)], local_sem.at[0])
    early.start()
    my_rows = pl.ds(pl.multiple_of(f * block, block), block)
    later = pl.ds(tile_rows, rows - tile_rows)
    own = pltpu.make_async_copy(x.at[f], mine.at[:, my_rows, later], local_sem.at[1])
    own.start()
    sends = []
    for i, j in others:
        copy = pltpu.make_async_remote_copy(
            src_ref=x.at[feat_peer(i, j)],
            dst_ref=mine.at[:, my_rows, later],
            send_sem=x_send.at[i * 4 + j],
            recv_sem=x_recv.at[i * 4 + j],
            device_id={"feat": feat_peer(i, j)},
            device_id_type=MESH,
        )
        copy.start()
        sends.append(copy)

    def turn(lo, size):
        def step(i, carry):
            at = pl.multiple_of(i * 128, 128)
            for p in range(2):
                to = pl.multiple_of(p * half_wide + i * 128, 128)
                turned[lo : lo + size, pl.ds(to, 128)] = mine[p, pl.ds(at, 128), lo : lo + size].T
            return carry

        lax.fori_loop(0, half_wide // 128, step, 0)

    def forward(lo, size):
        tile_of = lax.div(lax.broadcasted_iota(jnp.int32, (size, 256), 0) + lo, tile_rows)
        live = tile_of < live_count[0]

        def step(n, carry):
            at = pl.ds(pl.multiple_of(n * 256, 256), 256)
            pre = jnp.dot(turned[lo : lo + size], w[:, at], preferred_element_type=jnp.float32)
            pre = pre + bias[:, at]
            on = live & (pre > 0)
            act[lo : lo + size, at] = jnp.where(on, pre, 0.0).astype(act.dtype)
            c = cot[lo : lo + size, at].astype(jnp.float32)
            delta[lo : lo + size, at] = jnp.where(on, c, 0.0).astype(delta.dtype)
            return carry

        lax.fori_loop(0, hidden // 256, step, 0)

    early.wait()
    turn(0, tile_rows)
    w_own.wait()
    w_other.wait()
    forward(0, tile_rows)
    own.wait()
    for copy in sends:
        copy.wait()
    turn(tile_rows, rows - tile_rows)
    forward(tile_rows, rows - tile_rows)

    quarter = cols // 2

    def ours(h):
        return pl.ds(pl.multiple_of(core * cols + h * quarter, quarter), quarter)

    def theirs(h):
        return pl.ds(pl.multiple_of((1 - core) * cols + h * quarter, quarter), quarter)

    def product(p, at):
        return jnp.dot(mine[p], delta[:, at], preferred_element_type=jnp.float32)

    def remote(src, dst, send_sem, recv_sem, peer):
        copy = pltpu.make_async_remote_copy(
            src_ref=src, dst_ref=dst, send_sem=send_sem, recv_sem=recv_sem,
            device_id=peer, device_id_type=MESH,
        )
        copy.start()
        return copy

    def place(h, phase):
        return xx if (h + phase) % 2 == 0 else z

    def neighbour(h, phase, s):
        at = lax.rem(place(h, phase) + 4 + s, 4)
        return {"feat": z * 4 + at if (h + phase) % 2 == 0 else at * 4 + xx}

    phases = ((part_a, in_a), (part_b, in_b))
    started = {}

    def send_part(h, phase, p):
        part, arrived = (buffer.at[h] for buffer in phases[phase])
        for s in (2, 1, 3):
            m = (s - 1) * 2 + p
            started[h, phase, m] = remote(
                part.at[lax.rem(place(h, phase) + s, 4), p], arrived.at[s - 1, p],
                r_send.at[phase, h, m], r_recv.at[phase, h, m], neighbour(h, phase, s),
            )

    def gathered(h, phase, p):
        part, arrived = (buffer.at[h] for buffer in phases[phase])
        total = part[place(h, phase), p].astype(jnp.float32)
        for i in range(3):
            started[h, phase, i * 2 + p].wait_recv()
            total = total + arrived[i, p].astype(jnp.float32)
        return total

    order = ((0, 0), (1, 0), (0, 1), (1, 1))
    pairs = []
    for q, (h, p) in enumerate(order):
        other[q] = product(p, theirs(h)).astype(other.dtype)
        pairs.append(remote(other.at[q], pair_in.at[q], p_send.at[q], p_recv.at[q], partner))
    for q, (h, p) in enumerate(order):
        own_part = product(p, ours(h))
        pairs[q].wait_recv()
        own_part = (own_part + pair_in[q].astype(jnp.float32)).astype(part_a.dtype)
        for i in range(4):
            for j in range(4):
                rows_ij = own_part[(i * 4 + j) * block : (i * 4 + j + 1) * block]
                if h == 0:
                    part_a[h, j, p, i] = rows_ij
                else:
                    part_a[h, i, p, j] = rows_ij
        send_part(h, 0, p)
    for p in range(2):
        for h in range(2):
            reduced = gathered(h, 0, p).astype(part_b.dtype)
            for i in range(4):
                part_b[h, i, p] = reduced[i]
            send_part(h, 1, p)
    across = {}
    for h in range(2):
        for p in range(2):
            y_in[h, y, p] = gathered(h, 1, p).astype(y_in.dtype)
        for i in (2, 1, 3):
            across[h, i] = remote(
                y_in.at[h, y], y_in.at[h, y], y_send.at[h, i], y_recv.at[h, i], y_peer(i)
            )
    last = []
    for h in range(2):
        for i in range(1, 4):
            across[h, i].wait_recv()
        total = y_in[h, 0].astype(jnp.float32)
        for i in range(1, 4):
            total = total + y_in[h, i].astype(jnp.float32)
        half[h] = total
        last.append(remote(half.at[h], half_in.at[h], h_send.at[h], h_recv.at[h], partner))
        out_self[:, ours(h)] = half[h, 0]
        out_neigh[:, ours(h)] = half[h, 1]
    for h in range(2):
        last[h].wait_recv()
        out_self[:, theirs(h)] = half_in[h, 0]
        out_neigh[:, theirs(h)] = half_in[h, 1]
    for copy in [*pairs, *started.values(), *across.values(), *last]:
        copy.wait_send()


def layer(count, first, x, w_half, bias, cot):
    block, rows = x.shape[2], cot.shape[0]
    half_wide, hidden = w_half.shape
    quarter = hidden // 4
    bf16, f32 = jnp.bfloat16, jnp.float32
    vmem = pl.BlockSpec(memory_space=pltpu.VMEM)
    hbm = pl.BlockSpec(memory_space=pl.ANY)
    dma = pltpu.SemaphoreType.DMA
    return pl.pallas_call(
        layer_kernel,
        in_specs=[pl.BlockSpec(memory_space=pltpu.SMEM), hbm, hbm, hbm, vmem, vmem],
        out_specs=[vmem, vmem, vmem],
        out_shape=[
            jax.ShapeDtypeStruct((rows, hidden), bf16),
            jax.ShapeDtypeStruct((block, hidden), f32),
            jax.ShapeDtypeStruct((block, hidden), f32),
        ],
        scratch_shapes=[
            pltpu.VMEM((2 * half_wide, hidden), bf16),
            pltpu.VMEM((2, half_wide, rows), bf16),
            pltpu.VMEM((rows, 2 * half_wide), bf16),
            pltpu.VMEM((rows, hidden), bf16),
            pltpu.VMEM((4, half_wide, quarter), bf16),
            pltpu.VMEM((4, half_wide, quarter), bf16),
            pltpu.VMEM((2, 4, 2, 4, block, quarter), bf16),
            pltpu.VMEM((2, 3, 2, 4, block, quarter), bf16),
            pltpu.VMEM((2, 4, 2, block, quarter), bf16),
            pltpu.VMEM((2, 3, 2, block, quarter), bf16),
            pltpu.VMEM((2, 4, 2, block, quarter), bf16),
            pltpu.VMEM((2, 2, block, quarter), f32),
            pltpu.VMEM((2, 2, block, quarter), f32),
            dma((16,)), dma((16,)), dma((4,)), dma((4,)), dma((2, 2, 6)), dma((2, 2, 6)),
            dma((2, 4)), dma((2, 4)), dma((2,)), dma((2,)), dma((2,)), dma((3,)),
        ],
        compiler_params=pltpu.CompilerParams(
            collective_id=0, has_side_effects=True, vmem_limit_bytes=56 << 20
        ),
        cost_estimate=pl.CostEstimate(
            flops=2_500_000_000, bytes_accessed=10_000_000, transcendentals=0
        ),
    )(count, first, x, w_half, bias, cot)


def local(node_table, neighbor_ids, tile_counts, w_self, w_neigh, bias, cotangent):
    owned, rows, hidden = cotangent.shape
    ids = neighbor_ids.transpose(1, 0, 2)
    nodes, counts, first, w_half = first_tiles(tile_counts, ids, node_table, w_self, w_neigh)
    x = gather(counts, ids, nodes, node_table.shape[0])
    act, grad_self, grad_neigh = layer(
        tile_counts,
        first,
        x,
        w_half,
        bias.reshape(1, hidden),
        cotangent.reshape(owned * rows, hidden),
    )
    act, grad_self, grad_neigh = finish(act, grad_self, grad_neigh)
    return act.reshape(owned, rows, hidden), grad_self, grad_neigh


def solution(mesh):
    return jax.shard_map(
        local,
        mesh=mesh,
        in_specs=(
            P("feat", None),
            P("dp", None, None),
            P(("dp", "feat")),
            P("feat", None),
            P("feat", None),
            P(),
            P(("dp", "feat"), None, None),
        ),
        out_specs=(P(("dp", "feat"), None, None), P("feat", None), P("feat", None)),
        check_vma=False,
    )
```

```python
import jax
import jax.numpy as jnp
from jax import lax
from jax.experimental import pallas as pl
from jax.experimental.pallas import tpu as pltpu
from jax.sharding import PartitionSpec as P

MESH = pl.DeviceIdType.MESH
UNROLL = 32
BATCH = 8
CHUNK = 4096
LOADS = 8
SHARED = 8


def tile_sums(nodes, sums, ids, rows, block, base):
    lane_row = lax.broadcasted_iota(jnp.int32, (1, 128), 1)

    def group(g, carry):
        for u in range(UNROLL):
            r = g * UNROLL + u

            def node(k):
                return nodes[pl.ds(ids[k][base + r], 1), :]

            total = node(1)
            for k in range(2, len(ids)):
                total = total + node(k)
            sums[pl.ds(r, 1), :] = jnp.where(lane_row < block, node(0), total)
        return carry

    lax.fori_loop(0, rows // UNROLL, group, 0)
    held = sums[...]
    lane = lax.broadcasted_iota(jnp.int32, held.shape, 1)
    held = jnp.where(lane < block, held, held / (len(ids) - 1.0))
    return held.T.astype(jnp.bfloat16)


def first_kernel(
    count, ids_hbm, table_hbm, w_self, w_neigh, nodes, counts, first, weights,
    pair_counts, pair_ids, table, sums, sent, landed, got, w_got, got_pair, ids_pair, *rest
):
    fan, _, rows = ids_hbm.shape
    ids = (rest[:fan], rest[fan : 2 * fan])
    ids_sem, load_sem, c_send, c_recv, x_send, x_recv, w_send, w_recv, w_sem, i_send, i_recv = rest[
        2 * fan :
    ]
    d = lax.axis_index("dp")
    core = lax.rem(d, 2)
    partner = {"dp": d + 1 - 2 * core}
    block, width = table_hbm.shape
    peers = got.shape[0]
    f = lax.axis_index("feat")
    piece = width // LOADS

    def load(i):
        at = pl.ds(pl.multiple_of(i * piece, piece), piece)
        return pltpu.make_async_copy(table_hbm.at[:, at], table.at[:, at], load_sem.at[i])

    def peer(i):
        return lax.rem(f + i, peers)

    def fetch(i, slot, k):
        return pltpu.make_async_copy(
            ids_hbm.at[k, peer(i) * 3], ids[slot][k], ids_sem.at[slot, k]
        )

    for i in range(LOADS):
        load(i).start()
    for k in range(fan):
        fetch(1, 0, k).start()
    barrier = pltpu.get_barrier_semaphore()
    for i in range(1, peers):
        pl.semaphore_signal(barrier, inc=1, device_id={"feat": peer(i)}, device_id_type=MESH)
    pl.semaphore_signal(barrier, inc=1, device_id=partner, device_id_type=MESH)
    got[f] = jnp.zeros(got.shape[1:], jnp.int32) + count[0]

    def fill(i, carry):
        load(i).wait()

        def turn(j, inner):
            at = pl.multiple_of(i * piece + j * CHUNK, CHUNK)
            part = table[:, pl.ds(at, CHUNK)]
            wide = jnp.concatenate([part, part, jnp.zeros((128 - 2 * block, CHUNK), part.dtype)], 0)
            nodes[pl.ds(at, CHUNK), :] = wide.T.astype(jnp.float32)
            return inner

        lax.fori_loop(0, piece // CHUNK, turn, 0)
        return carry

    lax.fori_loop(0, 2, fill, 0)
    pl.semaphore_wait(barrier, peers)

    def count_copy(i):
        return pltpu.make_async_remote_copy(
            src_ref=got.at[f], dst_ref=got.at[f], send_sem=c_send.at[i], recv_sem=c_recv.at[i],
            device_id={"feat": peer(i)}, device_id_type=MESH,
        )

    my_rows = pl.ds(pl.multiple_of(f * block, block), block)

    def weight_copy(source, i):
        return pltpu.make_async_remote_copy(
            src_ref=source, dst_ref=w_got.at[my_rows], send_sem=w_send.at[i], recv_sem=w_recv.at[i],
            device_id={"feat": peer(i)}, device_id_type=MESH,
        )

    def tile_copy(i):
        return pltpu.make_async_remote_copy(
            src_ref=sent.at[peer(i)], dst_ref=landed.at[:, my_rows],
            send_sem=x_send.at[i], recv_sem=x_recv.at[i],
            device_id={"feat": peer(i)}, device_id_type=MESH,
        )

    for i in range(1, peers):
        count_copy(i).start()
    for which, source in enumerate((w_self, w_neigh)):

        @pl.when(core == which)
        def _():
            keep = pltpu.make_async_copy(source, w_got.at[my_rows], w_sem)
            keep.start()
            for i in range(1, peers):
                weight_copy(source, i).start()
            keep.wait()

    def ids_copy(c):
        return pltpu.make_async_remote_copy(
            src_ref=ids_hbm.at[:, 3 * (peers - SHARED + c) + 1], dst_ref=ids_pair.at[:, c],
            send_sem=i_send.at[c], recv_sem=i_recv.at[c], device_id=partner, device_id_type=MESH,
        )

    for c in range(SHARED):
        ids_copy(c).start()
    lax.fori_loop(2, LOADS, fill, 0)
    for i in range(1, peers):
        count_copy(i).wait()
    pair_copy = pltpu.make_async_remote_copy(
        src_ref=got, dst_ref=got_pair, send_sem=i_send.at[SHARED], recv_sem=i_recv.at[SHARED],
        device_id=partner, device_id_type=MESH,
    )
    pair_copy.start()

    def pair(p, carry):
        for slot in range(2):
            i = p * 2 + slot + 1
            for k in range(fan):
                fetch(i, slot, k).wait()
            if slot == 0:
                for k in range(fan):
                    fetch(i + 1, 1, k).start()
            else:

                @pl.when(i < peers)
                def _():
                    for k in range(fan):
                        fetch(i + 1, 0, k).start()

            turned = tile_sums(nodes, sums, ids[slot], rows, block, 0)
            for part in range(2):
                sent[peer(i), part] = turned[part * block : (part + 1) * block]

            @pl.when(i < peers)
            def _():
                tile_copy(i).start()

        return carry

    lax.fori_loop(0, peers // 2, pair, 0)
    for part in range(2):
        landed[part, my_rows] = sent[f, part]

    def settle(i, carry):
        tile_copy(i).wait()
        weight_copy(w_self, i).wait()
        return carry

    lax.fori_loop(1, peers, settle, 0)
    keep = pltpu.make_async_copy(w_got, weights, w_sem)
    keep.start()
    keep.wait()
    pair_copy.wait()
    for c in range(SHARED):
        ids_copy(c).wait()
    counts[...] = got[...]
    pair_counts[...] = got_pair[...]
    pair_ids[...] = ids_pair[...]
    first[...] = landed[...]


def first_tiles(count, ids, table, w_self, w_neigh):
    fan, tiles, rows = ids.shape
    block, width = table.shape
    hidden = w_self.shape[1]
    peers = tiles // 3
    dma = pltpu.SemaphoreType.DMA
    hbm = pl.BlockSpec(memory_space=pl.ANY)
    vmem = pl.BlockSpec(memory_space=pltpu.VMEM)
    nodes, *others = pl.pallas_call(
        first_kernel,
        in_specs=[pl.BlockSpec(memory_space=pltpu.SMEM), hbm, hbm, hbm, hbm],
        out_specs=[vmem, vmem, vmem, hbm, vmem, vmem],
        out_shape=[
            pltpu.VMEM((width, 128), jnp.float32),
            jax.ShapeDtypeStruct((peers, 1, 128), jnp.int32),
            jax.ShapeDtypeStruct((2, peers * block, rows), jnp.bfloat16),
            jax.ShapeDtypeStruct((peers * block, hidden), w_self.dtype),
            jax.ShapeDtypeStruct((peers, 1, 128), jnp.int32),
            jax.ShapeDtypeStruct((fan, SHARED, rows), jnp.int32),
        ],
        scratch_shapes=[
            pltpu.VMEM((block, width), table.dtype),
            pltpu.VMEM((rows, 128), jnp.float32),
            pltpu.VMEM((peers, 2, block, rows), jnp.bfloat16),
            pltpu.VMEM((2, peers * block, rows), jnp.bfloat16),
            pltpu.VMEM((peers, 1, 128), jnp.int32),
            pltpu.VMEM((peers * block, hidden), w_self.dtype),
            pltpu.VMEM((peers, 1, 128), jnp.int32),
            pltpu.VMEM((fan, SHARED, rows), jnp.int32),
        ]
        + [pltpu.SMEM((rows,), jnp.int32)] * (2 * fan)
        + [dma((2, fan)), dma((LOADS,))]
        + [dma((peers,))] * 6
        + [dma, dma((SHARED + 1,)), dma((SHARED + 1,))],
        compiler_params=pltpu.CompilerParams(
            collective_id=1, has_side_effects=True, vmem_limit_bytes=28 << 20
        ),
        cost_estimate=pl.CostEstimate(
            flops=60_000_000_000, bytes_accessed=150_000_000, transcendentals=0
        ),
    )(count, ids, table, w_self, w_neigh)
    return pltpu.with_memory_space_constraint(nodes, pltpu.VMEM), *others


def gather_kernel(counts, pair_counts, ids_hbm, pair_ids, nodes, out, helped, sums, given, *rest):
    fan, tiles, rows = ids_hbm.shape
    ids, sem = (rest[:fan], rest[fan : 2 * fan]), rest[2 * fan]
    block = out.shape[2]
    peers = tiles // 3
    flat = [[ref.reshape(BATCH * rows) for ref in refs] for refs in ids]

    def fetch(batch, slot, k):
        return pltpu.make_async_copy(
            ids_hbm.at[k, pl.ds(batch * BATCH, BATCH)], ids[slot][k], sem.at[slot, k]
        )

    for k in range(fan):
        fetch(0, 0, k).start()

    def pair_fetch(k):
        return pltpu.make_async_copy(pair_ids.at[k], ids[0][k], sem.at[0, k])

    def load_of(ref):
        return sum((ref[m, 0, 0] - 1 for m in range(peers)), jnp.int32(0))

    more = load_of(counts) - load_of(pair_counts)
    for side, (ref, surplus) in enumerate(((counts, more), (pair_counts, -more))):
        limit = lax.div(jnp.maximum(surplus, 0), 2)
        seen = jnp.int32(0)
        for c in range(SHARED):
            second = jnp.where(ref[peers - SHARED + c, 0, 0] >= 2, 1, 0)
            given[side * SHARED + c] = jnp.where(seen < limit, second, 0)
            seen = seen + second

    def one_batch(batch, slot):
        def tile(j, carry):
            t = batch * BATCH + j
            m, place = lax.div(t, 3), lax.rem(t, 3)
            away = given[jnp.maximum(m - (peers - SHARED), 0)]
            away = (away > 0) & (place == 1) & (m >= peers - SHARED)
            live = (place < counts[m, 0, 0]) & jnp.logical_not(away)
            at = pl.ds(pl.multiple_of(jnp.maximum(place - 1, 0) * rows, rows), rows)

            @pl.when(live & (place > 0))
            def _():
                turned = tile_sums(nodes, sums, flat[slot], rows, block, j * rows)
                out[m, 0, :, at] = turned[:block]
                out[m, 1, :, at] = turned[block : 2 * block]

            @pl.when(jnp.logical_not(live))
            def _():
                out[m, :, :, at] = jnp.zeros((2, block, rows), out.dtype)

            return carry

        lax.fori_loop(0, BATCH, tile, 0)

    batches = tiles // BATCH

    def pair(p, carry):
        for slot in range(2):
            batch = p * 2 + slot
            for k in range(fan):
                fetch(batch, slot, k).wait()
            if slot == 0:
                for k in range(fan):
                    fetch(batch + 1, 1, k).start()
            else:

                @pl.when(batch < batches - 1)
                def _():
                    for k in range(fan):
                        fetch(batch + 1, 0, k).start()

                @pl.when(batch == batches - 1)
                def _():
                    for k in range(fan):
                        pair_fetch(k).start()

            one_batch(batch, slot)
        return carry

    lax.fori_loop(0, batches // 2, pair, 0)
    for k in range(fan):
        pair_fetch(k).wait()

    def help_with(c, carry):
        taken = given[SHARED + c] > 0

        @pl.when(taken)
        def _():
            turned = tile_sums(nodes, sums, flat[0], rows, block, c * rows)
            helped[c, 0] = turned[:block]
            helped[c, 1] = turned[block : 2 * block]

        @pl.when(jnp.logical_not(taken))
        def _():
            helped[c] = jnp.zeros((2, block, rows), out.dtype)

        return carry

    lax.fori_loop(0, SHARED, help_with, 0)


def gather(counts, pair_counts, ids, pair_ids, nodes, block):
    fan, tiles, rows = ids.shape
    vmem = pl.BlockSpec(memory_space=pltpu.VMEM)
    return pl.pallas_call(
        gather_kernel,
        in_specs=[pl.BlockSpec(memory_space=pltpu.SMEM)] * 2
        + [pl.BlockSpec(memory_space=pl.ANY)] * 2
        + [vmem],
        out_specs=[vmem, vmem],
        scratch_shapes=[
            pltpu.VMEM((rows, 128), jnp.float32),
            pltpu.SMEM((2 * SHARED,), jnp.int32),
        ]
        + [pltpu.SMEM((BATCH, rows), jnp.int32)] * (2 * fan)
        + [pltpu.SemaphoreType.DMA((2, fan))],
        out_shape=[
            jax.ShapeDtypeStruct((tiles // 3, 2, block, 2 * rows), jnp.bfloat16),
            jax.ShapeDtypeStruct((SHARED, 2, block, rows), jnp.bfloat16),
        ],
        compiler_params=pltpu.CompilerParams(vmem_limit_bytes=28 << 20),
        cost_estimate=pl.CostEstimate(
            flops=60_000_000_000, bytes_accessed=150_000_000, transcendentals=0
        ),
    )(counts, pair_counts, ids, pair_ids, nodes)


def finish_kernel(a, b, c, out_a, out_b, out_c, held_a, held_b, held_c, sem):
    moves = []
    for q in range(4):
        at = pl.ds(q * (a.shape[0] // 4), a.shape[0] // 4)
        moves.append((a.at[at], held_a.at[at], out_a.at[at]))
    moves += [(b, held_b, out_b), (c, held_c, out_c)]
    ins = [pltpu.make_async_copy(x, h, sem.at[0, i]) for i, (x, h, _) in enumerate(moves)]
    outs = [pltpu.make_async_copy(h, o, sem.at[1, i]) for i, (_, h, o) in enumerate(moves)]
    for copy in ins:
        copy.start()
    for arrived, leaving in zip(ins, outs):
        arrived.wait()
        leaving.start()
    for copy in outs:
        copy.wait()


def finish(*arrays):
    return pl.pallas_call(
        finish_kernel,
        in_specs=[pl.BlockSpec(memory_space=pl.ANY)] * 3,
        out_specs=[pl.BlockSpec(memory_space=pl.ANY)] * 3,
        out_shape=[jax.ShapeDtypeStruct(x.shape, x.dtype) for x in arrays],
        scratch_shapes=[pltpu.VMEM(x.shape, x.dtype) for x in arrays]
        + [pltpu.SemaphoreType.DMA((2, 6))],
        compiler_params=pltpu.CompilerParams(vmem_limit_bytes=56 << 20),
    )(*arrays)


def layer_kernel(
    live_count, first, x, helped, w_half, bias, cot, act, out_self, out_neigh,
    w, mine, x_late, help_in, turned, delta, other, pair_in, part_a, in_a, part_b, in_b,
    y_in, half, half_in, x_send, x_recv, p_send, p_recv, r_send, r_recv, y_send, y_recv, h_send, h_recv, local_sem, w_sem, help_sem,
):
    f, d = lax.axis_index("feat"), lax.axis_index("dp")
    z, xx = lax.div(f, 4), lax.rem(f, 4)
    y, core = lax.div(d, 2), lax.rem(d, 2)
    partner = {"dp": y * 2 + (1 - core)}
    half_wide, rows = mine.shape[1:]
    block = x.shape[2]
    hidden = w.shape[1]
    cols = hidden // 2

    def feat_peer(i, j):
        return lax.rem(z + i, 4) * 4 + lax.rem(xx + j, 4)

    def y_peer(i):
        return {"dp": lax.rem(y + i, 4) * 2 + core}

    others = [(i, j) for i in range(4) for j in range(4) if (i, j) != (0, 0)]

    w_rows = pl.ds(pl.multiple_of(core * half_wide, half_wide), half_wide)
    w_own = pltpu.make_async_copy(w_half, w.at[w_rows], w_sem.at[0])
    w_own.start()

    barrier = pltpu.get_barrier_semaphore()
    for i, j in others:
        pl.semaphore_signal(barrier, inc=1, device_id={"feat": feat_peer(i, j)}, device_id_type=MESH)
    pl.semaphore_signal(barrier, inc=1, device_id=partner, device_id_type=MESH)
    for i in range(1, 4):
        pl.semaphore_signal(barrier, inc=1, device_id=y_peer(i), device_id_type=MESH)
    pl.semaphore_wait(barrier, 19)

    def remote(src, dst, send_sem, recv_sem, peer):
        copy = pltpu.make_async_remote_copy(
            src_ref=src, dst_ref=dst, send_sem=send_sem, recv_sem=recv_sem,
            device_id=peer, device_id_type=MESH,
        )
        copy.start()
        return copy

    w_other = pltpu.make_async_remote_copy(
        src_ref=w_half, dst_ref=w.at[w_rows], send_sem=w_sem.at[1], recv_sem=w_sem.at[2],
        device_id=partner, device_id_type=MESH,
    )
    w_other.start()
    tile_rows = rows // 3
    early = pltpu.make_async_copy(first, mine.at[:, :, pl.ds(0, tile_rows)], local_sem.at[0])
    early.start()
    my_rows = pl.ds(pl.multiple_of(f * block, block), block)
    later = pl.ds(tile_rows, rows - tile_rows)
    early_peers = x.shape[0] - SHARED
    help_copy = remote(helped, help_in, help_sem.at[0], help_sem.at[1], partner)
    hold = pltpu.make_async_copy(x.at[pl.ds(early_peers, SHARED)], x_late, help_sem.at[2])
    hold.start()

    def own_copy(source):
        return pltpu.make_async_copy(source, mine.at[:, my_rows, later], local_sem.at[1])

    def send_copy(i, j, source):
        return pltpu.make_async_remote_copy(
            src_ref=source,
            dst_ref=mine.at[:, my_rows, later],
            send_sem=x_send.at[i * 4 + j],
            recv_sem=x_recv.at[i * 4 + j],
            device_id={"feat": feat_peer(i, j)},
            device_id_type=MESH,
        )

    @pl.when(f < early_peers)
    def _():
        own_copy(x.at[f]).start()

    for i, j in others:
        peer = feat_peer(i, j)

        @pl.when(peer < early_peers)
        def _():
            send_copy(i, j, x.at[peer]).start()

    hold.wait()
    help_copy.wait()
    x_late[:, :, :, :tile_rows] = x_late[:, :, :, :tile_rows] + help_in[...]

    @pl.when(f >= early_peers)
    def _():
        own_copy(x_late.at[f - early_peers]).start()

    for i, j in others:
        peer = feat_peer(i, j)

        @pl.when(peer >= early_peers)
        def _():
            send_copy(i, j, x_late.at[peer - early_peers]).start()

    def turn(lo, size):
        def step(i, carry):
            at = pl.multiple_of(i * 128, 128)
            for p in range(2):
                to = pl.multiple_of(p * half_wide + i * 128, 128)
                turned[lo : lo + size, pl.ds(to, 128)] = mine[p, pl.ds(at, 128), lo : lo + size].T
            return carry

        lax.fori_loop(0, half_wide // 128, step, 0)

    def forward(lo, size):
        tile_of = lax.div(lax.broadcasted_iota(jnp.int32, (size, 256), 0) + lo, tile_rows)
        live = tile_of < live_count[0]

        def step(n, carry):
            at = pl.ds(pl.multiple_of(n * 256, 256), 256)
            pre = jnp.dot(turned[lo : lo + size], w[:, at], preferred_element_type=jnp.float32)
            pre = pre + bias[:, at]
            on = live & (pre > 0)
            act[lo : lo + size, at] = jnp.where(on, pre, 0.0).astype(act.dtype)
            c = cot[lo : lo + size, at].astype(jnp.float32)
            delta[lo : lo + size, at] = jnp.where(on, c, 0.0).astype(delta.dtype)
            return carry

        lax.fori_loop(0, hidden // 256, step, 0)

    early.wait()
    turn(0, tile_rows)
    w_own.wait()
    w_other.wait()
    forward(0, tile_rows)
    own_copy(x.at[f]).wait()
    for i, j in others:
        send_copy(i, j, x.at[feat_peer(i, j)]).wait()
    turn(tile_rows, rows - tile_rows)
    forward(tile_rows, rows - tile_rows)

    quarter = cols // 2

    def ours(h):
        return pl.ds(pl.multiple_of(core * cols + h * quarter, quarter), quarter)

    def theirs(h):
        return pl.ds(pl.multiple_of((1 - core) * cols + h * quarter, quarter), quarter)

    def product(p, at):
        return jnp.dot(mine[p], delta[:, at], preferred_element_type=jnp.float32)

    def place(h, phase):
        return xx if (h + phase) % 2 == 0 else z

    def neighbour(h, phase, s):
        at = lax.rem(place(h, phase) + 4 + s, 4)
        return {"feat": z * 4 + at if (h + phase) % 2 == 0 else at * 4 + xx}

    phases = ((part_a, in_a), (part_b, in_b))
    started = {}

    def send_part(h, phase, p):
        part, arrived = (buffer.at[h] for buffer in phases[phase])
        for s in (2, 1, 3):
            m = (s - 1) * 2 + p
            started[h, phase, m] = remote(
                part.at[lax.rem(place(h, phase) + s, 4), p], arrived.at[s - 1, p],
                r_send.at[phase, h, m], r_recv.at[phase, h, m], neighbour(h, phase, s),
            )

    def gathered(h, phase, p):
        part, arrived = (buffer.at[h] for buffer in phases[phase])
        total = part[place(h, phase), p].astype(jnp.float32)
        for i in range(3):
            started[h, phase, i * 2 + p].wait_recv()
            total = total + arrived[i, p].astype(jnp.float32)
        return total

    order = ((0, 0), (1, 0), (0, 1), (1, 1))
    pairs = []
    for q, (h, p) in enumerate(order):
        other[q] = product(p, theirs(h)).astype(other.dtype)
        pairs.append(remote(other.at[q], pair_in.at[q], p_send.at[q], p_recv.at[q], partner))
    for q, (h, p) in enumerate(order):
        own_part = product(p, ours(h))
        pairs[q].wait_recv()
        own_part = (own_part + pair_in[q].astype(jnp.float32)).astype(part_a.dtype)
        for i in range(4):
            for j in range(4):
                rows_ij = own_part[(i * 4 + j) * block : (i * 4 + j + 1) * block]
                if h == 0:
                    part_a[h, j, p, i] = rows_ij
                else:
                    part_a[h, i, p, j] = rows_ij
        send_part(h, 0, p)
    for p in range(2):
        for h in range(2):
            reduced = gathered(h, 0, p).astype(part_b.dtype)
            for i in range(4):
                part_b[h, i, p] = reduced[i]
            send_part(h, 1, p)
    across = {}
    for h in range(2):
        for p in range(2):
            y_in[h, y, p] = gathered(h, 1, p).astype(y_in.dtype)
        for i in (2, 1, 3):
            across[h, i] = remote(
                y_in.at[h, y], y_in.at[h, y], y_send.at[h, i], y_recv.at[h, i], y_peer(i)
            )
    last = []
    for h in range(2):
        for i in range(1, 4):
            across[h, i].wait_recv()
        total = y_in[h, 0].astype(jnp.float32)
        for i in range(1, 4):
            total = total + y_in[h, i].astype(jnp.float32)
        half[h] = total
        last.append(remote(half.at[h], half_in.at[h], h_send.at[h], h_recv.at[h], partner))
        out_self[:, ours(h)] = half[h, 0]
        out_neigh[:, ours(h)] = half[h, 1]
    for h in range(2):
        last[h].wait_recv()
        out_self[:, theirs(h)] = half_in[h, 0]
        out_neigh[:, theirs(h)] = half_in[h, 1]
    for copy in [*pairs, *started.values(), *across.values(), *last]:
        copy.wait_send()


def layer(count, first, x, helped, w_half, bias, cot):
    block, rows = x.shape[2], cot.shape[0]
    half_wide, hidden = w_half.shape
    quarter = hidden // 4
    bf16, f32 = jnp.bfloat16, jnp.float32
    vmem = pl.BlockSpec(memory_space=pltpu.VMEM)
    hbm = pl.BlockSpec(memory_space=pl.ANY)
    dma = pltpu.SemaphoreType.DMA
    return pl.pallas_call(
        layer_kernel,
        in_specs=[pl.BlockSpec(memory_space=pltpu.SMEM), hbm, hbm, hbm, hbm, vmem, vmem],
        out_specs=[vmem, vmem, vmem],
        out_shape=[
            jax.ShapeDtypeStruct((rows, hidden), bf16),
            jax.ShapeDtypeStruct((block, hidden), f32),
            jax.ShapeDtypeStruct((block, hidden), f32),
        ],
        scratch_shapes=[
            pltpu.VMEM((2 * half_wide, hidden), bf16),
            pltpu.VMEM((2, half_wide, rows), bf16),
            pltpu.VMEM((SHARED, 2, block, 2 * rows // 3), bf16),
            pltpu.VMEM((SHARED, 2, block, rows // 3), bf16),
            pltpu.VMEM((rows, 2 * half_wide), bf16),
            pltpu.VMEM((rows, hidden), bf16),
            pltpu.VMEM((4, half_wide, quarter), bf16),
            pltpu.VMEM((4, half_wide, quarter), bf16),
            pltpu.VMEM((2, 4, 2, 4, block, quarter), bf16),
            pltpu.VMEM((2, 3, 2, 4, block, quarter), bf16),
            pltpu.VMEM((2, 4, 2, block, quarter), bf16),
            pltpu.VMEM((2, 3, 2, block, quarter), bf16),
            pltpu.VMEM((2, 4, 2, block, quarter), bf16),
            pltpu.VMEM((2, 2, block, quarter), f32),
            pltpu.VMEM((2, 2, block, quarter), f32),
            dma((16,)), dma((16,)), dma((4,)), dma((4,)), dma((2, 2, 6)), dma((2, 2, 6)),
            dma((2, 4)), dma((2, 4)), dma((2,)), dma((2,)), dma((2,)), dma((3,)), dma((3,)),
        ],
        compiler_params=pltpu.CompilerParams(
            collective_id=0, has_side_effects=True, vmem_limit_bytes=56 << 20
        ),
        cost_estimate=pl.CostEstimate(
            flops=2_500_000_000, bytes_accessed=10_000_000, transcendentals=0
        ),
    )(count, first, x, helped, w_half, bias, cot)


def local(node_table, neighbor_ids, tile_counts, w_self, w_neigh, bias, cotangent):
    owned, rows, hidden = cotangent.shape
    ids = neighbor_ids.transpose(1, 0, 2)
    nodes, counts, first, w_half, pair_counts, pair_ids = first_tiles(
        tile_counts, ids, node_table, w_self, w_neigh
    )
    x, helped = gather(counts, pair_counts, ids, pair_ids, nodes, node_table.shape[0])
    act, grad_self, grad_neigh = layer(
        tile_counts,
        first,
        x,
        helped,
        w_half,
        bias.reshape(1, hidden),
        cotangent.reshape(owned * rows, hidden),
    )
    act, grad_self, grad_neigh = finish(act, grad_self, grad_neigh)
    return act.reshape(owned, rows, hidden), grad_self, grad_neigh


def solution(mesh):
    return jax.shard_map(
        local,
        mesh=mesh,
        in_specs=(
            P("feat", None),
            P("dp", None, None),
            P(("dp", "feat")),
            P("feat", None),
            P("feat", None),
            P(),
            P(("dp", "feat"), None, None),
        ),
        out_specs=(P(("dp", "feat"), None, None), P("feat", None), P("feat", None)),
        check_vma=False,
    )
```

```python
import jax
import jax.numpy as jnp
from jax import lax
from jax.experimental import pallas as pl
from jax.experimental.pallas import tpu as pltpu
from jax.sharding import PartitionSpec as P

MESH = pl.DeviceIdType.MESH
UNROLL = 32
BATCH = 8
CHUNK = 4096
LOADS = 8
SHARED = 8


def tile_sums(nodes, sums, ids, rows, block, base):
    lane_row = lax.broadcasted_iota(jnp.int32, (1, 128), 1)

    def group(g, carry):
        for u in range(UNROLL):
            r = g * UNROLL + u

            def node(k):
                return nodes[pl.ds(ids[k][base + r], 1), :]

            total = node(1)
            for k in range(2, len(ids)):
                total = total + node(k)
            sums[pl.ds(r, 1), :] = jnp.where(lane_row < block, node(0), total)
        return carry

    lax.fori_loop(0, rows // UNROLL, group, 0)
    held = sums[...]
    lane = lax.broadcasted_iota(jnp.int32, held.shape, 1)
    held = jnp.where(lane < block, held, held / (len(ids) - 1.0))
    return held.T.astype(jnp.bfloat16)


def first_kernel(
    count, ids_hbm, table_hbm, w_self, w_neigh, nodes, counts, first, weights,
    pair_counts, pair_ids, table, sums, sent, landed, got, w_got, got_pair, ids_pair, *rest
):
    fan, _, rows = ids_hbm.shape
    ids = (rest[:fan], rest[fan : 2 * fan])
    ids_sem, load_sem, c_send, c_recv, x_send, x_recv, w_send, w_recv, w_sem, i_send, i_recv = rest[
        2 * fan :
    ]
    d = lax.axis_index("dp")
    core = lax.rem(d, 2)
    partner = {"dp": d + 1 - 2 * core}
    block, width = table_hbm.shape
    peers = got.shape[0]
    f = lax.axis_index("feat")
    piece = width // LOADS

    def load(i):
        at = pl.ds(pl.multiple_of(i * piece, piece), piece)
        return pltpu.make_async_copy(table_hbm.at[:, at], table.at[:, at], load_sem.at[i])

    def peer(i):
        return lax.rem(f + i, peers)

    def fetch(i, slot, k):
        return pltpu.make_async_copy(
            ids_hbm.at[k, peer(i) * 3], ids[slot][k], ids_sem.at[slot, k]
        )

    for i in range(LOADS):
        load(i).start()
    for k in range(fan):
        fetch(1, 0, k).start()
    barrier = pltpu.get_barrier_semaphore()
    for i in range(1, peers):
        pl.semaphore_signal(barrier, inc=1, device_id={"feat": peer(i)}, device_id_type=MESH)
    pl.semaphore_signal(barrier, inc=1, device_id=partner, device_id_type=MESH)
    got[f] = jnp.zeros(got.shape[1:], jnp.int32) + count[0]

    def fill(i, carry):
        load(i).wait()

        def turn(j, inner):
            at = pl.multiple_of(i * piece + j * CHUNK, CHUNK)
            part = table[:, pl.ds(at, CHUNK)]
            wide = jnp.concatenate([part, part, jnp.zeros((128 - 2 * block, CHUNK), part.dtype)], 0)
            nodes[pl.ds(at, CHUNK), :] = wide.T.astype(jnp.float32)
            return inner

        lax.fori_loop(0, piece // CHUNK, turn, 0)
        return carry

    lax.fori_loop(0, 2, fill, 0)
    pl.semaphore_wait(barrier, peers)

    def count_copy(i):
        return pltpu.make_async_remote_copy(
            src_ref=got.at[f], dst_ref=got.at[f], send_sem=c_send.at[i], recv_sem=c_recv.at[i],
            device_id={"feat": peer(i)}, device_id_type=MESH,
        )

    my_rows = pl.ds(pl.multiple_of(f * block, block), block)

    def weight_copy(source, i):
        return pltpu.make_async_remote_copy(
            src_ref=source, dst_ref=w_got.at[my_rows], send_sem=w_send.at[i], recv_sem=w_recv.at[i],
            device_id={"feat": peer(i)}, device_id_type=MESH,
        )

    def tile_copy(i):
        return pltpu.make_async_remote_copy(
            src_ref=sent.at[peer(i)], dst_ref=landed.at[:, my_rows],
            send_sem=x_send.at[i], recv_sem=x_recv.at[i],
            device_id={"feat": peer(i)}, device_id_type=MESH,
        )

    for i in range(1, peers):
        count_copy(i).start()
    for which, source in enumerate((w_self, w_neigh)):

        @pl.when(core == which)
        def _():
            keep = pltpu.make_async_copy(source, w_got.at[my_rows], w_sem)
            keep.start()
            for i in range(1, peers):
                weight_copy(source, i).start()
            keep.wait()

    def ids_copy(c):
        return pltpu.make_async_remote_copy(
            src_ref=ids_hbm.at[:, 3 * (peers - SHARED + c) + 1], dst_ref=ids_pair.at[:, c],
            send_sem=i_send.at[c], recv_sem=i_recv.at[c], device_id=partner, device_id_type=MESH,
        )

    for c in range(SHARED):
        ids_copy(c).start()
    lax.fori_loop(2, LOADS, fill, 0)
    pair_copy = pltpu.make_async_remote_copy(
        src_ref=got, dst_ref=got_pair, send_sem=i_send.at[SHARED], recv_sem=i_recv.at[SHARED],
        device_id=partner, device_id_type=MESH,
    )

    def pair(p, carry):
        @pl.when(p == 5)
        def _():
            for i in range(1, peers):
                count_copy(i).wait()
            pair_copy.start()

        for slot in range(2):
            i = p * 2 + slot + 1
            for k in range(fan):
                fetch(i, slot, k).wait()
            if slot == 0:
                for k in range(fan):
                    fetch(i + 1, 1, k).start()
            else:

                @pl.when(i < peers)
                def _():
                    for k in range(fan):
                        fetch(i + 1, 0, k).start()

            turned = tile_sums(nodes, sums, ids[slot], rows, block, 0)
            for part in range(2):
                sent[peer(i), part] = turned[part * block : (part + 1) * block]

            @pl.when(i < peers)
            def _():
                tile_copy(i).start()

        return carry

    lax.fori_loop(0, peers // 2, pair, 0)
    for part in range(2):
        landed[part, my_rows] = sent[f, part]

    def settle(i, carry):
        tile_copy(i).wait()
        weight_copy(w_self, i).wait()
        return carry

    lax.fori_loop(1, peers, settle, 0)
    keep = pltpu.make_async_copy(w_got, weights, w_sem)
    keep.start()
    keep.wait()
    pair_copy.wait()
    for c in range(SHARED):
        ids_copy(c).wait()
    counts[...] = got[...]
    pair_counts[...] = got_pair[...]
    pair_ids[...] = ids_pair[...]
    first[...] = landed[...]


def first_tiles(count, ids, table, w_self, w_neigh):
    fan, tiles, rows = ids.shape
    block, width = table.shape
    hidden = w_self.shape[1]
    peers = tiles // 3
    dma = pltpu.SemaphoreType.DMA
    hbm = pl.BlockSpec(memory_space=pl.ANY)
    vmem = pl.BlockSpec(memory_space=pltpu.VMEM)
    nodes, *others = pl.pallas_call(
        first_kernel,
        in_specs=[pl.BlockSpec(memory_space=pltpu.SMEM), hbm, hbm, hbm, hbm],
        out_specs=[vmem, vmem, vmem, hbm, vmem, vmem],
        out_shape=[
            pltpu.VMEM((width, 128), jnp.float32),
            jax.ShapeDtypeStruct((peers, 1, 128), jnp.int32),
            jax.ShapeDtypeStruct((2, peers * block, rows), jnp.bfloat16),
            jax.ShapeDtypeStruct((peers * block, hidden), w_self.dtype),
            jax.ShapeDtypeStruct((peers, 1, 128), jnp.int32),
            jax.ShapeDtypeStruct((fan, SHARED, rows), jnp.int32),
        ],
        scratch_shapes=[
            pltpu.VMEM((block, width), table.dtype),
            pltpu.VMEM((rows, 128), jnp.float32),
            pltpu.VMEM((peers, 2, block, rows), jnp.bfloat16),
            pltpu.VMEM((2, peers * block, rows), jnp.bfloat16),
            pltpu.VMEM((peers, 1, 128), jnp.int32),
            pltpu.VMEM((peers * block, hidden), w_self.dtype),
            pltpu.VMEM((peers, 1, 128), jnp.int32),
            pltpu.VMEM((fan, SHARED, rows), jnp.int32),
        ]
        + [pltpu.SMEM((rows,), jnp.int32)] * (2 * fan)
        + [dma((2, fan)), dma((LOADS,))]
        + [dma((peers,))] * 6
        + [dma, dma((SHARED + 1,)), dma((SHARED + 1,))],
        compiler_params=pltpu.CompilerParams(
            collective_id=1, has_side_effects=True, vmem_limit_bytes=28 << 20
        ),
        cost_estimate=pl.CostEstimate(
            flops=60_000_000_000, bytes_accessed=150_000_000, transcendentals=0
        ),
    )(count, ids, table, w_self, w_neigh)
    return pltpu.with_memory_space_constraint(nodes, pltpu.VMEM), *others


def gather_kernel(counts, pair_counts, ids_hbm, pair_ids, nodes, out, helped, sums, given, *rest):
    fan, tiles, rows = ids_hbm.shape
    ids, sem = (rest[:fan], rest[fan : 2 * fan]), rest[2 * fan]
    block = out.shape[2]
    peers = tiles // 3
    flat = [[ref.reshape(BATCH * rows) for ref in refs] for refs in ids]

    def fetch(batch, slot, k):
        return pltpu.make_async_copy(
            ids_hbm.at[k, pl.ds(batch * BATCH, BATCH)], ids[slot][k], sem.at[slot, k]
        )

    for k in range(fan):
        fetch(0, 0, k).start()

    def pair_fetch(k):
        return pltpu.make_async_copy(pair_ids.at[k], ids[0][k], sem.at[0, k])

    def load_of(ref):
        return sum((ref[m, 0, 0] - 1 for m in range(peers)), jnp.int32(0))

    more = load_of(counts) - load_of(pair_counts)
    for side, (ref, surplus) in enumerate(((counts, more), (pair_counts, -more))):
        limit = lax.div(jnp.maximum(surplus, 0), 2)
        seen = jnp.int32(0)
        for c in range(SHARED):
            second = jnp.where(ref[peers - SHARED + c, 0, 0] >= 2, 1, 0)
            given[side * SHARED + c] = jnp.where(seen < limit, second, 0)
            seen = seen + second

    def one_batch(batch, slot):
        def tile(j, carry):
            t = batch * BATCH + j
            m, place = lax.div(t, 3), lax.rem(t, 3)
            away = given[jnp.maximum(m - (peers - SHARED), 0)]
            away = (away > 0) & (place == 1) & (m >= peers - SHARED)
            live = (place < counts[m, 0, 0]) & jnp.logical_not(away)
            at = pl.ds(pl.multiple_of(jnp.maximum(place - 1, 0) * rows, rows), rows)

            @pl.when(live & (place > 0))
            def _():
                turned = tile_sums(nodes, sums, flat[slot], rows, block, j * rows)
                out[m, 0, :, at] = turned[:block]
                out[m, 1, :, at] = turned[block : 2 * block]

            @pl.when(jnp.logical_not(live))
            def _():
                out[m, :, :, at] = jnp.zeros((2, block, rows), out.dtype)

            return carry

        lax.fori_loop(0, BATCH, tile, 0)

    batches = tiles // BATCH

    def pair(p, carry):
        for slot in range(2):
            batch = p * 2 + slot
            for k in range(fan):
                fetch(batch, slot, k).wait()
            if slot == 0:
                for k in range(fan):
                    fetch(batch + 1, 1, k).start()
            else:

                @pl.when(batch < batches - 1)
                def _():
                    for k in range(fan):
                        fetch(batch + 1, 0, k).start()

                @pl.when(batch == batches - 1)
                def _():
                    for k in range(fan):
                        pair_fetch(k).start()

            one_batch(batch, slot)
        return carry

    lax.fori_loop(0, batches // 2, pair, 0)
    for k in range(fan):
        pair_fetch(k).wait()

    def help_with(c, carry):
        taken = given[SHARED + c] > 0

        @pl.when(taken)
        def _():
            turned = tile_sums(nodes, sums, flat[0], rows, block, c * rows)
            helped[c, 0] = turned[:block]
            helped[c, 1] = turned[block : 2 * block]

        @pl.when(jnp.logical_not(taken))
        def _():
            helped[c] = jnp.zeros((2, block, rows), out.dtype)

        return carry

    lax.fori_loop(0, SHARED, help_with, 0)


def gather(counts, pair_counts, ids, pair_ids, nodes, block):
    fan, tiles, rows = ids.shape
    vmem = pl.BlockSpec(memory_space=pltpu.VMEM)
    return pl.pallas_call(
        gather_kernel,
        in_specs=[pl.BlockSpec(memory_space=pltpu.SMEM)] * 2
        + [pl.BlockSpec(memory_space=pl.ANY)] * 2
        + [vmem],
        out_specs=[vmem, vmem],
        scratch_shapes=[
            pltpu.VMEM((rows, 128), jnp.float32),
            pltpu.SMEM((2 * SHARED,), jnp.int32),
        ]
        + [pltpu.SMEM((BATCH, rows), jnp.int32)] * (2 * fan)
        + [pltpu.SemaphoreType.DMA((2, fan))],
        out_shape=[
            jax.ShapeDtypeStruct((tiles // 3, 2, block, 2 * rows), jnp.bfloat16),
            jax.ShapeDtypeStruct((SHARED, 2, block, rows), jnp.bfloat16),
        ],
        compiler_params=pltpu.CompilerParams(vmem_limit_bytes=28 << 20),
        cost_estimate=pl.CostEstimate(
            flops=60_000_000_000, bytes_accessed=150_000_000, transcendentals=0
        ),
    )(counts, pair_counts, ids, pair_ids, nodes)


def finish_kernel(a, b, c, out_a, out_b, out_c, held_a, held_b, held_c, sem):
    moves = []
    for q in range(4):
        at = pl.ds(q * (a.shape[0] // 4), a.shape[0] // 4)
        moves.append((a.at[at], held_a.at[at], out_a.at[at]))
    moves += [(b, held_b, out_b), (c, held_c, out_c)]
    ins = [pltpu.make_async_copy(x, h, sem.at[0, i]) for i, (x, h, _) in enumerate(moves)]
    outs = [pltpu.make_async_copy(h, o, sem.at[1, i]) for i, (_, h, o) in enumerate(moves)]
    for copy in ins:
        copy.start()
    for arrived, leaving in zip(ins, outs):
        arrived.wait()
        leaving.start()
    for copy in outs:
        copy.wait()


def finish(*arrays):
    return pl.pallas_call(
        finish_kernel,
        in_specs=[pl.BlockSpec(memory_space=pl.ANY)] * 3,
        out_specs=[pl.BlockSpec(memory_space=pl.ANY)] * 3,
        out_shape=[jax.ShapeDtypeStruct(x.shape, x.dtype) for x in arrays],
        scratch_shapes=[pltpu.VMEM(x.shape, x.dtype) for x in arrays]
        + [pltpu.SemaphoreType.DMA((2, 6))],
        compiler_params=pltpu.CompilerParams(vmem_limit_bytes=56 << 20),
    )(*arrays)


def layer_kernel(
    live_count, first, x, helped, w_half, bias, cot, act, out_self, out_neigh,
    w, mine, x_late, help_in, turned, delta, other, pair_in, part_a, in_a, part_b, in_b,
    y_in, half, half_in, x_send, x_recv, p_send, p_recv, r_send, r_recv, y_send, y_recv, h_send, h_recv, local_sem, w_sem, help_sem,
    l_send, l_recv,
):
    f, d = lax.axis_index("feat"), lax.axis_index("dp")
    z, xx = lax.div(f, 4), lax.rem(f, 4)
    y, core = lax.div(d, 2), lax.rem(d, 2)
    partner = {"dp": y * 2 + (1 - core)}
    half_wide, rows = mine.shape[1:]
    block = x.shape[2]
    hidden = w.shape[1]
    cols = hidden // 2

    def feat_peer(i, j):
        return lax.rem(z + i, 4) * 4 + lax.rem(xx + j, 4)

    def y_peer(i):
        return {"dp": lax.rem(y + i, 4) * 2 + core}

    others = [(i, j) for i in range(4) for j in range(4) if (i, j) != (0, 0)]

    w_rows = pl.ds(pl.multiple_of(core * half_wide, half_wide), half_wide)
    w_own = pltpu.make_async_copy(w_half, w.at[w_rows], w_sem.at[0])
    w_own.start()

    barrier = pltpu.get_barrier_semaphore()
    for i, j in others:
        pl.semaphore_signal(barrier, inc=1, device_id={"feat": feat_peer(i, j)}, device_id_type=MESH)
    pl.semaphore_signal(barrier, inc=1, device_id=partner, device_id_type=MESH)
    for i in range(1, 4):
        pl.semaphore_signal(barrier, inc=1, device_id=y_peer(i), device_id_type=MESH)
    pl.semaphore_wait(barrier, 19)

    def remote(src, dst, send_sem, recv_sem, peer):
        copy = pltpu.make_async_remote_copy(
            src_ref=src, dst_ref=dst, send_sem=send_sem, recv_sem=recv_sem,
            device_id=peer, device_id_type=MESH,
        )
        copy.start()
        return copy

    w_other = pltpu.make_async_remote_copy(
        src_ref=w_half, dst_ref=w.at[w_rows], send_sem=w_sem.at[1], recv_sem=w_sem.at[2],
        device_id=partner, device_id_type=MESH,
    )
    w_other.start()
    tile_rows = rows // 3
    early = pltpu.make_async_copy(first, mine.at[:, :, pl.ds(0, tile_rows)], local_sem.at[0])
    early.start()
    my_rows = pl.ds(pl.multiple_of(f * block, block), block)
    both, second = pl.ds(tile_rows, 2 * tile_rows), pl.ds(tile_rows, tile_rows)
    third = pl.ds(2 * tile_rows, tile_rows)
    tail = pl.ds(tile_rows, tile_rows)
    early_peers = x.shape[0] - SHARED
    help_copy = remote(helped, help_in, help_sem.at[0], help_sem.at[1], partner)
    hold = pltpu.make_async_copy(
        x.at[pl.ds(early_peers, SHARED), :, :, pl.ds(0, tile_rows)], x_late, help_sem.at[2]
    )
    hold.start()

    def own_copy(source, at, which):
        return pltpu.make_async_copy(source, mine.at[:, my_rows, at], local_sem.at[which])

    def send_copy(i, j, source, at, sems):
        return pltpu.make_async_remote_copy(
            src_ref=source,
            dst_ref=mine.at[:, my_rows, at],
            send_sem=sems[0].at[i * 4 + j],
            recv_sem=sems[1].at[i * 4 + j],
            device_id={"feat": feat_peer(i, j)},
            device_id_type=MESH,
        )

    def whole(i, j):
        return send_copy(i, j, x.at[feat_peer(i, j)], both, (x_send, x_recv))

    def last_tile(i, j):
        return send_copy(i, j, x.at[feat_peer(i, j), :, :, tail], third, (x_send, x_recv))

    def shared_tile(i, j):
        place_of = jnp.maximum(feat_peer(i, j) - early_peers, 0)
        return send_copy(i, j, x_late.at[place_of], second, (l_send, l_recv))

    def by_peer(peer, early_do, late_do):
        pl.when(peer < early_peers)(early_do)
        pl.when(peer >= early_peers)(late_do)

    own_late = jnp.maximum(f - early_peers, 0)
    by_peer(
        f,
        lambda: own_copy(x.at[f], both, 1).start(),
        lambda: own_copy(x.at[f, :, :, tail], third, 1).start(),
    )
    for i, j in others:
        by_peer(
            feat_peer(i, j), lambda: whole(i, j).start(), lambda: last_tile(i, j).start()
        )
    hold.wait()
    help_copy.wait()
    x_late[...] = x_late[...] + help_in[...]
    pl.when(f >= early_peers)(lambda: own_copy(x_late.at[own_late], second, 2).start())
    for i, j in others:
        pl.when(feat_peer(i, j) >= early_peers)(lambda: shared_tile(i, j).start())

    def turn(lo, size):
        def step(i, carry):
            at = pl.multiple_of(i * 128, 128)
            for p in range(2):
                to = pl.multiple_of(p * half_wide + i * 128, 128)
                turned[lo : lo + size, pl.ds(to, 128)] = mine[p, pl.ds(at, 128), lo : lo + size].T
            return carry

        lax.fori_loop(0, half_wide // 128, step, 0)

    def forward(lo, size):
        tile_of = lax.div(lax.broadcasted_iota(jnp.int32, (size, 256), 0) + lo, tile_rows)
        live = tile_of < live_count[0]

        def step(n, carry):
            at = pl.ds(pl.multiple_of(n * 256, 256), 256)
            pre = jnp.dot(turned[lo : lo + size], w[:, at], preferred_element_type=jnp.float32)
            pre = pre + bias[:, at]
            on = live & (pre > 0)
            act[lo : lo + size, at] = jnp.where(on, pre, 0.0).astype(act.dtype)
            c = cot[lo : lo + size, at].astype(jnp.float32)
            delta[lo : lo + size, at] = jnp.where(on, c, 0.0).astype(delta.dtype)
            return carry

        lax.fori_loop(0, hidden // 256, step, 0)

    early.wait()
    turn(0, tile_rows)
    w_own.wait()
    w_other.wait()
    forward(0, tile_rows)

    def settle_early():
        own_copy(x.at[f], both, 1).wait()
        for i, j in others:
            whole(i, j).wait_recv()

    def settle_late():
        own_copy(x.at[f, :, :, tail], third, 1).wait()
        own_copy(x_late.at[own_late], second, 2).wait()
        for i, j in others:
            last_tile(i, j).wait_recv()
            shared_tile(i, j).wait_recv()

    def sent_late(i, j):
        last_tile(i, j).wait_send()
        shared_tile(i, j).wait_send()

    by_peer(f, settle_early, settle_late)
    turn(tile_rows, rows - tile_rows)
    forward(tile_rows, rows - tile_rows)

    quarter = cols // 2

    def ours(h):
        return pl.ds(pl.multiple_of(core * cols + h * quarter, quarter), quarter)

    def theirs(h):
        return pl.ds(pl.multiple_of((1 - core) * cols + h * quarter, quarter), quarter)

    def product(p, at):
        return jnp.dot(mine[p], delta[:, at], preferred_element_type=jnp.float32)

    def place(h, phase):
        return xx if (h + phase) % 2 == 0 else z

    def neighbour(h, phase, s):
        at = lax.rem(place(h, phase) + 4 + s, 4)
        return {"feat": z * 4 + at if (h + phase) % 2 == 0 else at * 4 + xx}

    phases = ((part_a, in_a), (part_b, in_b))
    started = {}

    def send_part(h, phase, p):
        part, arrived = (buffer.at[h] for buffer in phases[phase])
        for s in (2, 1, 3):
            m = (s - 1) * 2 + p
            started[h, phase, m] = remote(
                part.at[lax.rem(place(h, phase) + s, 4), p], arrived.at[s - 1, p],
                r_send.at[phase, h, m], r_recv.at[phase, h, m], neighbour(h, phase, s),
            )

    def gathered(h, phase, p):
        part, arrived = (buffer.at[h] for buffer in phases[phase])
        total = part[place(h, phase), p].astype(jnp.float32)
        for i in range(3):
            started[h, phase, i * 2 + p].wait_recv()
            total = total + arrived[i, p].astype(jnp.float32)
        return total

    order = ((0, 0), (1, 0), (0, 1), (1, 1))
    pairs = []
    for q, (h, p) in enumerate(order):
        other[q] = product(p, theirs(h)).astype(other.dtype)
        pairs.append(remote(other.at[q], pair_in.at[q], p_send.at[q], p_recv.at[q], partner))
    for q, (h, p) in enumerate(order):
        own_part = product(p, ours(h))
        pairs[q].wait_recv()
        own_part = (own_part + pair_in[q].astype(jnp.float32)).astype(part_a.dtype)
        for i in range(4):
            for j in range(4):
                rows_ij = own_part[(i * 4 + j) * block : (i * 4 + j + 1) * block]
                if h == 0:
                    part_a[h, j, p, i] = rows_ij
                else:
                    part_a[h, i, p, j] = rows_ij
        send_part(h, 0, p)
    for p in range(2):
        for h in range(2):
            reduced = gathered(h, 0, p).astype(part_b.dtype)
            for i in range(4):
                part_b[h, i, p] = reduced[i]
            send_part(h, 1, p)
    across = {}
    for h in range(2):
        for p in range(2):
            y_in[h, y, p] = gathered(h, 1, p).astype(y_in.dtype)
        for i in (2, 1, 3):
            across[h, i] = remote(
                y_in.at[h, y], y_in.at[h, y], y_send.at[h, i], y_recv.at[h, i], y_peer(i)
            )
    last = []
    for h in range(2):
        for i in range(1, 4):
            across[h, i].wait_recv()
        total = y_in[h, 0].astype(jnp.float32)
        for i in range(1, 4):
            total = total + y_in[h, i].astype(jnp.float32)
        half[h] = total
        last.append(remote(half.at[h], half_in.at[h], h_send.at[h], h_recv.at[h], partner))
        out_self[:, ours(h)] = half[h, 0]
        out_neigh[:, ours(h)] = half[h, 1]
    for h in range(2):
        last[h].wait_recv()
        out_self[:, theirs(h)] = half_in[h, 0]
        out_neigh[:, theirs(h)] = half_in[h, 1]
    for copy in [*pairs, *started.values(), *across.values(), *last]:
        copy.wait_send()
    for i, j in others:
        by_peer(feat_peer(i, j), lambda: whole(i, j).wait_send(), lambda: sent_late(i, j))


def layer(count, first, x, helped, w_half, bias, cot):
    block, rows = x.shape[2], cot.shape[0]
    half_wide, hidden = w_half.shape
    quarter = hidden // 4
    bf16, f32 = jnp.bfloat16, jnp.float32
    vmem = pl.BlockSpec(memory_space=pltpu.VMEM)
    hbm = pl.BlockSpec(memory_space=pl.ANY)
    dma = pltpu.SemaphoreType.DMA
    return pl.pallas_call(
        layer_kernel,
        in_specs=[pl.BlockSpec(memory_space=pltpu.SMEM), hbm, hbm, hbm, hbm, vmem, vmem],
        out_specs=[vmem, vmem, vmem],
        out_shape=[
            jax.ShapeDtypeStruct((rows, hidden), bf16),
            jax.ShapeDtypeStruct((block, hidden), f32),
            jax.ShapeDtypeStruct((block, hidden), f32),
        ],
        scratch_shapes=[
            pltpu.VMEM((2 * half_wide, hidden), bf16),
            pltpu.VMEM((2, half_wide, rows), bf16),
            pltpu.VMEM((SHARED, 2, block, rows // 3), bf16),
            pltpu.VMEM((SHARED, 2, block, rows // 3), bf16),
            pltpu.VMEM((rows, 2 * half_wide), bf16),
            pltpu.VMEM((rows, hidden), bf16),
            pltpu.VMEM((4, half_wide, quarter), bf16),
            pltpu.VMEM((4, half_wide, quarter), bf16),
            pltpu.VMEM((2, 4, 2, 4, block, quarter), bf16),
            pltpu.VMEM((2, 3, 2, 4, block, quarter), bf16),
            pltpu.VMEM((2, 4, 2, block, quarter), bf16),
            pltpu.VMEM((2, 3, 2, block, quarter), bf16),
            pltpu.VMEM((2, 4, 2, block, quarter), bf16),
            pltpu.VMEM((2, 2, block, quarter), f32),
            pltpu.VMEM((2, 2, block, quarter), f32),
            dma((16,)), dma((16,)), dma((4,)), dma((4,)), dma((2, 2, 6)), dma((2, 2, 6)),
            dma((2, 4)), dma((2, 4)), dma((2,)), dma((2,)), dma((3,)), dma((3,)), dma((3,)),
            dma((16,)), dma((16,)),
        ],
        compiler_params=pltpu.CompilerParams(
            collective_id=0, has_side_effects=True, vmem_limit_bytes=56 << 20
        ),
        cost_estimate=pl.CostEstimate(
            flops=2_500_000_000, bytes_accessed=10_000_000, transcendentals=0
        ),
    )(count, first, x, helped, w_half, bias, cot)


def local(node_table, neighbor_ids, tile_counts, w_self, w_neigh, bias, cotangent):
    owned, rows, hidden = cotangent.shape
    ids = neighbor_ids.transpose(1, 0, 2)
    nodes, counts, first, w_half, pair_counts, pair_ids = first_tiles(
        tile_counts, ids, node_table, w_self, w_neigh
    )
    x, helped = gather(counts, pair_counts, ids, pair_ids, nodes, node_table.shape[0])
    act, grad_self, grad_neigh = layer(
        tile_counts,
        first,
        x,
        helped,
        w_half,
        bias.reshape(1, hidden),
        cotangent.reshape(owned * rows, hidden),
    )
    act, grad_self, grad_neigh = finish(act, grad_self, grad_neigh)
    return act.reshape(owned, rows, hidden), grad_self, grad_neigh


def solution(mesh):
    return jax.shard_map(
        local,
        mesh=mesh,
        in_specs=(
            P("feat", None),
            P("dp", None, None),
            P(("dp", "feat")),
            P("feat", None),
            P("feat", None),
            P(),
            P(("dp", "feat"), None, None),
        ),
        out_specs=(P(("dp", "feat"), None, None), P("feat", None), P("feat", None)),
        check_vma=False,
    )
```

```python
import jax
import jax.numpy as jnp
from jax import lax
from jax.experimental import pallas as pl
from jax.experimental.pallas import tpu as pltpu
from jax.sharding import PartitionSpec as P

MESH = pl.DeviceIdType.MESH
UNROLL = 32
BATCH = 8
CHUNK = 4096
LOADS = 8
SHARED = 8


def tile_sums(nodes, sums, ids, rows, block, base, unroll):
    lane_row = lax.broadcasted_iota(jnp.int32, (1, 128), 1)

    def group(g, carry):
        for u in range(unroll):
            r = g * unroll + u

            def node(k):
                return nodes[pl.ds(ids[k][base + r], 1), :]

            total = node(1)
            for k in range(2, len(ids)):
                total = total + node(k)
            sums[pl.ds(r, 1), :] = jnp.where(lane_row < block, node(0), total)
        return carry

    lax.fori_loop(0, rows // unroll, group, 0)
    held = sums[...]
    lane = lax.broadcasted_iota(jnp.int32, held.shape, 1)
    held = jnp.where(lane < block, held, held / (len(ids) - 1.0))
    return held.T.astype(jnp.bfloat16)


def first_kernel(
    count, ids_hbm, table_hbm, w_self, w_neigh, nodes, counts, first, weights,
    pair_counts, pair_ids, table, sums, sent, landed, got, w_got, got_pair, ids_pair, *rest
):
    fan, _, rows = ids_hbm.shape
    ids = (rest[:fan], rest[fan : 2 * fan])
    ids_sem, load_sem, c_send, c_recv, x_send, x_recv, w_send, w_recv, w_sem, i_send, i_recv = rest[
        2 * fan :
    ]
    d = lax.axis_index("dp")
    core = lax.rem(d, 2)
    partner = {"dp": d + 1 - 2 * core}
    block, width = table_hbm.shape
    peers = got.shape[0]
    f = lax.axis_index("feat")
    piece = width // LOADS

    def load(i):
        at = pl.ds(pl.multiple_of(i * piece, piece), piece)
        return pltpu.make_async_copy(table_hbm.at[:, at], table.at[:, at], load_sem.at[i])

    def peer(i):
        return lax.rem(f + i, peers)

    def fetch(i, slot, k):
        return pltpu.make_async_copy(
            ids_hbm.at[k, peer(i) * 3], ids[slot][k], ids_sem.at[slot, k]
        )

    for i in range(LOADS):
        load(i).start()
    for k in range(fan):
        fetch(1, 0, k).start()
    barrier = pltpu.get_barrier_semaphore()
    for i in range(1, peers):
        pl.semaphore_signal(barrier, inc=1, device_id={"feat": peer(i)}, device_id_type=MESH)
    pl.semaphore_signal(barrier, inc=1, device_id=partner, device_id_type=MESH)
    got[f] = jnp.zeros(got.shape[1:], jnp.int32) + count[0]

    def fill(i, carry):
        load(i).wait()

        def turn(j, inner):
            at = pl.multiple_of(i * piece + j * CHUNK, CHUNK)
            part = table[:, pl.ds(at, CHUNK)]
            wide = jnp.concatenate([part, part, jnp.zeros((128 - 2 * block, CHUNK), part.dtype)], 0)
            nodes[pl.ds(at, CHUNK), :] = wide.T.astype(jnp.float32)
            return inner

        lax.fori_loop(0, piece // CHUNK, turn, 0)
        return carry

    lax.fori_loop(0, 2, fill, 0)
    pl.semaphore_wait(barrier, peers)

    def count_copy(i):
        return pltpu.make_async_remote_copy(
            src_ref=got.at[f], dst_ref=got.at[f], send_sem=c_send.at[i], recv_sem=c_recv.at[i],
            device_id={"feat": peer(i)}, device_id_type=MESH,
        )

    my_rows = pl.ds(pl.multiple_of(f * block, block), block)

    def weight_copy(source, i):
        return pltpu.make_async_remote_copy(
            src_ref=source, dst_ref=w_got.at[my_rows], send_sem=w_send.at[i], recv_sem=w_recv.at[i],
            device_id={"feat": peer(i)}, device_id_type=MESH,
        )

    def tile_copy(i):
        return pltpu.make_async_remote_copy(
            src_ref=sent.at[peer(i)], dst_ref=landed.at[:, my_rows],
            send_sem=x_send.at[i], recv_sem=x_recv.at[i],
            device_id={"feat": peer(i)}, device_id_type=MESH,
        )

    for i in range(1, peers):
        count_copy(i).start()
    for which, source in enumerate((w_self, w_neigh)):

        @pl.when(core == which)
        def _():
            keep = pltpu.make_async_copy(source, w_got.at[my_rows], w_sem)
            keep.start()
            for i in range(1, peers):
                weight_copy(source, i).start()
            keep.wait()

    def ids_copy(c):
        return pltpu.make_async_remote_copy(
            src_ref=ids_hbm.at[:, 3 * (peers - SHARED + c) + 1], dst_ref=ids_pair.at[:, c],
            send_sem=i_send.at[c], recv_sem=i_recv.at[c], device_id=partner, device_id_type=MESH,
        )

    for c in range(SHARED):
        ids_copy(c).start()
    lax.fori_loop(2, LOADS, fill, 0)
    pair_copy = pltpu.make_async_remote_copy(
        src_ref=got, dst_ref=got_pair, send_sem=i_send.at[SHARED], recv_sem=i_recv.at[SHARED],
        device_id=partner, device_id_type=MESH,
    )

    def pair(p, carry):
        @pl.when(p == 5)
        def _():
            for i in range(1, peers):
                count_copy(i).wait()
            pair_copy.start()

        for slot in range(2):
            i = p * 2 + slot + 1
            for k in range(fan):
                fetch(i, slot, k).wait()
            if slot == 0:
                for k in range(fan):
                    fetch(i + 1, 1, k).start()
            else:

                @pl.when(i < peers)
                def _():
                    for k in range(fan):
                        fetch(i + 1, 0, k).start()

            turned = tile_sums(nodes, sums, ids[slot], rows, block, 0, UNROLL)
            for part in range(2):
                sent[peer(i), part] = turned[part * block : (part + 1) * block]

            @pl.when(i < peers)
            def _():
                tile_copy(i).start()

        return carry

    lax.fori_loop(0, peers // 2, pair, 0)
    for part in range(2):
        landed[part, my_rows] = sent[f, part]

    def settle(i, carry):
        tile_copy(i).wait()
        weight_copy(w_self, i).wait()
        return carry

    lax.fori_loop(1, peers, settle, 0)
    keep = pltpu.make_async_copy(w_got, weights, w_sem)
    keep.start()
    keep.wait()
    pair_copy.wait()
    for c in range(SHARED):
        ids_copy(c).wait()
    counts[...] = got[...]
    pair_counts[...] = got_pair[...]
    pair_ids[...] = ids_pair[...]
    first[...] = landed[...]


def first_tiles(count, ids, table, w_self, w_neigh):
    fan, tiles, rows = ids.shape
    block, width = table.shape
    hidden = w_self.shape[1]
    peers = tiles // 3
    dma = pltpu.SemaphoreType.DMA
    hbm = pl.BlockSpec(memory_space=pl.ANY)
    vmem = pl.BlockSpec(memory_space=pltpu.VMEM)
    nodes, *others = pl.pallas_call(
        first_kernel,
        in_specs=[pl.BlockSpec(memory_space=pltpu.SMEM), hbm, hbm, hbm, hbm],
        out_specs=[vmem, vmem, vmem, hbm, vmem, vmem],
        out_shape=[
            pltpu.VMEM((width, 128), jnp.float32),
            jax.ShapeDtypeStruct((peers, 1, 128), jnp.int32),
            jax.ShapeDtypeStruct((2, peers * block, rows), jnp.bfloat16),
            jax.ShapeDtypeStruct((peers * block, hidden), w_self.dtype),
            jax.ShapeDtypeStruct((peers, 1, 128), jnp.int32),
            jax.ShapeDtypeStruct((fan, SHARED, rows), jnp.int32),
        ],
        scratch_shapes=[
            pltpu.VMEM((block, width), table.dtype),
            pltpu.VMEM((rows, 128), jnp.float32),
            pltpu.VMEM((peers, 2, block, rows), jnp.bfloat16),
            pltpu.VMEM((2, peers * block, rows), jnp.bfloat16),
            pltpu.VMEM((peers, 1, 128), jnp.int32),
            pltpu.VMEM((peers * block, hidden), w_self.dtype),
            pltpu.VMEM((peers, 1, 128), jnp.int32),
            pltpu.VMEM((fan, SHARED, rows), jnp.int32),
        ]
        + [pltpu.SMEM((rows,), jnp.int32)] * (2 * fan)
        + [dma((2, fan)), dma((LOADS,))]
        + [dma((peers,))] * 6
        + [dma, dma((SHARED + 1,)), dma((SHARED + 1,))],
        compiler_params=pltpu.CompilerParams(
            collective_id=1, has_side_effects=True, vmem_limit_bytes=28 << 20
        ),
        cost_estimate=pl.CostEstimate(
            flops=60_000_000_000, bytes_accessed=150_000_000, transcendentals=0
        ),
    )(count, ids, table, w_self, w_neigh)
    return pltpu.with_memory_space_constraint(nodes, pltpu.VMEM), *others


def gather_kernel(counts, pair_counts, ids_hbm, pair_ids, nodes, out, helped, sums, given, *rest):
    fan, tiles, rows = ids_hbm.shape
    ids, sem = (rest[:fan], rest[fan : 2 * fan]), rest[2 * fan]
    block = out.shape[2]
    peers = tiles // 3
    flat = [[ref.reshape(BATCH * rows) for ref in refs] for refs in ids]

    def fetch(batch, slot, k):
        return pltpu.make_async_copy(
            ids_hbm.at[k, pl.ds(batch * BATCH, BATCH)], ids[slot][k], sem.at[slot, k]
        )

    for k in range(fan):
        fetch(0, 0, k).start()

    def pair_fetch(k):
        return pltpu.make_async_copy(pair_ids.at[k], ids[0][k], sem.at[0, k])

    def load_of(ref):
        return sum((ref[m, 0, 0] - 1 for m in range(peers)), jnp.int32(0))

    more = load_of(counts) - load_of(pair_counts)
    for side, (ref, surplus) in enumerate(((counts, more), (pair_counts, -more))):
        limit = lax.div(jnp.maximum(surplus, 0), 2)
        seen = jnp.int32(0)
        for c in range(SHARED):
            second = jnp.where(ref[peers - SHARED + c, 0, 0] >= 2, 1, 0)
            given[side * SHARED + c] = jnp.where(seen < limit, second, 0)
            seen = seen + second

    def one_batch(batch, slot):
        def tile(j, carry):
            t = batch * BATCH + j
            m, place = lax.div(t, 3), lax.rem(t, 3)
            away = given[jnp.maximum(m - (peers - SHARED), 0)]
            away = (away > 0) & (place == 1) & (m >= peers - SHARED)
            live = (place < counts[m, 0, 0]) & jnp.logical_not(away)
            at = pl.ds(pl.multiple_of(jnp.maximum(place - 1, 0) * rows, rows), rows)

            @pl.when(live & (place > 0))
            def _():
                turned = tile_sums(nodes, sums, flat[slot], rows, block, j * rows, rows)
                out[m, 0, :, at] = turned[:block]
                out[m, 1, :, at] = turned[block : 2 * block]

            @pl.when(jnp.logical_not(live))
            def _():
                out[m, :, :, at] = jnp.zeros((2, block, rows), out.dtype)

            return carry

        lax.fori_loop(0, BATCH, tile, 0)

    batches = tiles // BATCH

    def pair(p, carry):
        for slot in range(2):
            batch = p * 2 + slot
            for k in range(fan):
                fetch(batch, slot, k).wait()
            if slot == 0:
                for k in range(fan):
                    fetch(batch + 1, 1, k).start()
            else:

                @pl.when(batch < batches - 1)
                def _():
                    for k in range(fan):
                        fetch(batch + 1, 0, k).start()

                @pl.when(batch == batches - 1)
                def _():
                    for k in range(fan):
                        pair_fetch(k).start()

            one_batch(batch, slot)
        return carry

    lax.fori_loop(0, batches // 2, pair, 0)
    for k in range(fan):
        pair_fetch(k).wait()

    def help_with(c, carry):
        taken = given[SHARED + c] > 0

        @pl.when(taken)
        def _():
            turned = tile_sums(nodes, sums, flat[0], rows, block, c * rows, UNROLL)
            helped[c, 0] = turned[:block]
            helped[c, 1] = turned[block : 2 * block]

        @pl.when(jnp.logical_not(taken))
        def _():
            helped[c] = jnp.zeros((2, block, rows), out.dtype)

        return carry

    lax.fori_loop(0, SHARED, help_with, 0)


def gather(counts, pair_counts, ids, pair_ids, nodes, block):
    fan, tiles, rows = ids.shape
    vmem = pl.BlockSpec(memory_space=pltpu.VMEM)
    return pl.pallas_call(
        gather_kernel,
        in_specs=[pl.BlockSpec(memory_space=pltpu.SMEM)] * 2
        + [pl.BlockSpec(memory_space=pl.ANY)] * 2
        + [vmem],
        out_specs=[vmem, vmem],
        scratch_shapes=[
            pltpu.VMEM((rows, 128), jnp.float32),
            pltpu.SMEM((2 * SHARED,), jnp.int32),
        ]
        + [pltpu.SMEM((BATCH, rows), jnp.int32)] * (2 * fan)
        + [pltpu.SemaphoreType.DMA((2, fan))],
        out_shape=[
            jax.ShapeDtypeStruct((tiles // 3, 2, block, 2 * rows), jnp.bfloat16),
            jax.ShapeDtypeStruct((SHARED, 2, block, rows), jnp.bfloat16),
        ],
        compiler_params=pltpu.CompilerParams(vmem_limit_bytes=28 << 20),
        cost_estimate=pl.CostEstimate(
            flops=60_000_000_000, bytes_accessed=150_000_000, transcendentals=0
        ),
    )(counts, pair_counts, ids, pair_ids, nodes)


def finish_kernel(a, b, c, out_a, out_b, out_c, held_a, held_b, held_c, sem):
    moves = []
    for q in range(4):
        at = pl.ds(q * (a.shape[0] // 4), a.shape[0] // 4)
        moves.append((a.at[at], held_a.at[at], out_a.at[at]))
    moves += [(b, held_b, out_b), (c, held_c, out_c)]
    ins = [pltpu.make_async_copy(x, h, sem.at[0, i]) for i, (x, h, _) in enumerate(moves)]
    outs = [pltpu.make_async_copy(h, o, sem.at[1, i]) for i, (_, h, o) in enumerate(moves)]
    for copy in ins:
        copy.start()
    for arrived, leaving in zip(ins, outs):
        arrived.wait()
        leaving.start()
    for copy in outs:
        copy.wait()


def finish(*arrays):
    return pl.pallas_call(
        finish_kernel,
        in_specs=[pl.BlockSpec(memory_space=pl.ANY)] * 3,
        out_specs=[pl.BlockSpec(memory_space=pl.ANY)] * 3,
        out_shape=[jax.ShapeDtypeStruct(x.shape, x.dtype) for x in arrays],
        scratch_shapes=[pltpu.VMEM(x.shape, x.dtype) for x in arrays]
        + [pltpu.SemaphoreType.DMA((2, 6))],
        compiler_params=pltpu.CompilerParams(vmem_limit_bytes=56 << 20),
    )(*arrays)


def layer_kernel(
    live_count, first, x, helped, w_half, bias, cot, act, out_self, out_neigh,
    w, mine, x_late, help_in, turned, delta, other, pair_in, part_a, in_a, part_b, in_b,
    y_in, half, half_in, x_send, x_recv, p_send, p_recv, r_send, r_recv, y_send, y_recv, h_send, h_recv, local_sem, w_sem, help_sem,
    l_send, l_recv,
):
    f, d = lax.axis_index("feat"), lax.axis_index("dp")
    z, xx = lax.div(f, 4), lax.rem(f, 4)
    y, core = lax.div(d, 2), lax.rem(d, 2)
    partner = {"dp": y * 2 + (1 - core)}
    half_wide, rows = mine.shape[1:]
    block = x.shape[2]
    hidden = w.shape[1]
    cols = hidden // 2

    def feat_peer(i, j):
        return lax.rem(z + i, 4) * 4 + lax.rem(xx + j, 4)

    def y_peer(i):
        return {"dp": lax.rem(y + i, 4) * 2 + core}

    others = [(i, j) for i in range(4) for j in range(4) if (i, j) != (0, 0)]

    w_rows = pl.ds(pl.multiple_of(core * half_wide, half_wide), half_wide)
    w_own = pltpu.make_async_copy(w_half, w.at[w_rows], w_sem.at[0])
    w_own.start()

    barrier = pltpu.get_barrier_semaphore()
    for i, j in others:
        pl.semaphore_signal(barrier, inc=1, device_id={"feat": feat_peer(i, j)}, device_id_type=MESH)
    pl.semaphore_signal(barrier, inc=1, device_id=partner, device_id_type=MESH)
    for i in range(1, 4):
        pl.semaphore_signal(barrier, inc=1, device_id=y_peer(i), device_id_type=MESH)
    pl.semaphore_wait(barrier, 19)

    def remote(src, dst, send_sem, recv_sem, peer):
        copy = pltpu.make_async_remote_copy(
            src_ref=src, dst_ref=dst, send_sem=send_sem, recv_sem=recv_sem,
            device_id=peer, device_id_type=MESH,
        )
        copy.start()
        return copy

    w_other = pltpu.make_async_remote_copy(
        src_ref=w_half, dst_ref=w.at[w_rows], send_sem=w_sem.at[1], recv_sem=w_sem.at[2],
        device_id=partner, device_id_type=MESH,
    )
    w_other.start()
    tile_rows = rows // 3
    early = pltpu.make_async_copy(first, mine.at[:, :, pl.ds(0, tile_rows)], local_sem.at[0])
    early.start()
    my_rows = pl.ds(pl.multiple_of(f * block, block), block)
    both, second = pl.ds(tile_rows, 2 * tile_rows), pl.ds(tile_rows, tile_rows)
    third = pl.ds(2 * tile_rows, tile_rows)
    tail = pl.ds(tile_rows, tile_rows)
    early_peers = x.shape[0] - SHARED
    help_copy = remote(helped, help_in, help_sem.at[0], help_sem.at[1], partner)
    hold = pltpu.make_async_copy(
        x.at[pl.ds(early_peers, SHARED), :, :, pl.ds(0, tile_rows)], x_late, help_sem.at[2]
    )
    hold.start()

    def own_copy(source, at, which):
        return pltpu.make_async_copy(source, mine.at[:, my_rows, at], local_sem.at[which])

    def send_copy(i, j, source, at, sems):
        return pltpu.make_async_remote_copy(
            src_ref=source,
            dst_ref=mine.at[:, my_rows, at],
            send_sem=sems[0].at[i * 4 + j],
            recv_sem=sems[1].at[i * 4 + j],
            device_id={"feat": feat_peer(i, j)},
            device_id_type=MESH,
        )

    def whole(i, j):
        return send_copy(i, j, x.at[feat_peer(i, j)], both, (x_send, x_recv))

    def last_tile(i, j):
        return send_copy(i, j, x.at[feat_peer(i, j), :, :, tail], third, (x_send, x_recv))

    def shared_tile(i, j):
        place_of = jnp.maximum(feat_peer(i, j) - early_peers, 0)
        return send_copy(i, j, x_late.at[place_of], second, (l_send, l_recv))

    def by_peer(peer, early_do, late_do):
        pl.when(peer < early_peers)(early_do)
        pl.when(peer >= early_peers)(late_do)

    own_late = jnp.maximum(f - early_peers, 0)
    by_peer(
        f,
        lambda: own_copy(x.at[f], both, 1).start(),
        lambda: own_copy(x.at[f, :, :, tail], third, 1).start(),
    )
    for i, j in others:
        by_peer(
            feat_peer(i, j), lambda: whole(i, j).start(), lambda: last_tile(i, j).start()
        )
    hold.wait()
    help_copy.wait()
    x_late[...] = x_late[...] + help_in[...]
    pl.when(f >= early_peers)(lambda: own_copy(x_late.at[own_late], second, 2).start())
    for i, j in others:
        pl.when(feat_peer(i, j) >= early_peers)(lambda: shared_tile(i, j).start())

    def turn(lo, size):
        def step(i, carry):
            at = pl.multiple_of(i * 128, 128)
            for p in range(2):
                to = pl.multiple_of(p * half_wide + i * 128, 128)
                turned[lo : lo + size, pl.ds(to, 128)] = mine[p, pl.ds(at, 128), lo : lo + size].T
            return carry

        lax.fori_loop(0, half_wide // 128, step, 0)

    def forward(lo, size):
        tile_of = lax.div(lax.broadcasted_iota(jnp.int32, (size, 256), 0) + lo, tile_rows)
        live = tile_of < live_count[0]

        def step(n, carry):
            at = pl.ds(pl.multiple_of(n * 256, 256), 256)
            pre = jnp.dot(turned[lo : lo + size], w[:, at], preferred_element_type=jnp.float32)
            pre = pre + bias[:, at]
            on = live & (pre > 0)
            act[lo : lo + size, at] = jnp.where(on, pre, 0.0).astype(act.dtype)
            c = cot[lo : lo + size, at].astype(jnp.float32)
            delta[lo : lo + size, at] = jnp.where(on, c, 0.0).astype(delta.dtype)
            return carry

        lax.fori_loop(0, hidden // 256, step, 0)

    early.wait()
    turn(0, tile_rows)
    w_own.wait()
    w_other.wait()
    forward(0, tile_rows)

    def settle_early():
        own_copy(x.at[f], both, 1).wait()
        for i, j in others:
            whole(i, j).wait_recv()

    def settle_late():
        own_copy(x.at[f, :, :, tail], third, 1).wait()
        own_copy(x_late.at[own_late], second, 2).wait()
        for i, j in others:
            last_tile(i, j).wait_recv()
            shared_tile(i, j).wait_recv()

    def sent_late(i, j):
        last_tile(i, j).wait_send()
        shared_tile(i, j).wait_send()

    by_peer(f, settle_early, settle_late)
    turn(tile_rows, rows - tile_rows)
    forward(tile_rows, rows - tile_rows)

    quarter = cols // 2

    def ours(h):
        return pl.ds(pl.multiple_of(core * cols + h * quarter, quarter), quarter)

    def theirs(h):
        return pl.ds(pl.multiple_of((1 - core) * cols + h * quarter, quarter), quarter)

    def product(p, at):
        return jnp.dot(mine[p], delta[:, at], preferred_element_type=jnp.float32)

    def place(h, phase):
        return xx if (h + phase) % 2 == 0 else z

    def neighbour(h, phase, s):
        at = lax.rem(place(h, phase) + 4 + s, 4)
        return {"feat": z * 4 + at if (h + phase) % 2 == 0 else at * 4 + xx}

    phases = ((part_a, in_a), (part_b, in_b))
    started = {}

    def send_part(h, phase, p):
        part, arrived = (buffer.at[h] for buffer in phases[phase])
        for s in (2, 1, 3):
            m = (s - 1) * 2 + p
            started[h, phase, m] = remote(
                part.at[lax.rem(place(h, phase) + s, 4), p], arrived.at[s - 1, p],
                r_send.at[phase, h, m], r_recv.at[phase, h, m], neighbour(h, phase, s),
            )

    def gathered(h, phase, p):
        part, arrived = (buffer.at[h] for buffer in phases[phase])
        total = part[place(h, phase), p].astype(jnp.float32)
        for i in range(3):
            started[h, phase, i * 2 + p].wait_recv()
            total = total + arrived[i, p].astype(jnp.float32)
        return total

    order = ((0, 0), (1, 0), (0, 1), (1, 1))
    pairs = []
    for q, (h, p) in enumerate(order):
        other[q] = product(p, theirs(h)).astype(other.dtype)
        pairs.append(remote(other.at[q], pair_in.at[q], p_send.at[q], p_recv.at[q], partner))
    for q, (h, p) in enumerate(order):
        own_part = product(p, ours(h))
        pairs[q].wait_recv()
        own_part = (own_part + pair_in[q].astype(jnp.float32)).astype(part_a.dtype)
        for i in range(4):
            for j in range(4):
                rows_ij = own_part[(i * 4 + j) * block : (i * 4 + j + 1) * block]
                if h == 0:
                    part_a[h, j, p, i] = rows_ij
                else:
                    part_a[h, i, p, j] = rows_ij
        send_part(h, 0, p)
    for p in range(2):
        for h in range(2):
            reduced = gathered(h, 0, p).astype(part_b.dtype)
            for i in range(4):
                part_b[h, i, p] = reduced[i]
            send_part(h, 1, p)
    across = {}
    for h in range(2):
        for p in range(2):
            y_in[h, y, p] = gathered(h, 1, p).astype(y_in.dtype)
        for i in (2, 1, 3):
            across[h, i] = remote(
                y_in.at[h, y], y_in.at[h, y], y_send.at[h, i], y_recv.at[h, i], y_peer(i)
            )
    last = []
    for h in range(2):
        for i in range(1, 4):
            across[h, i].wait_recv()
        total = y_in[h, 0].astype(jnp.float32)
        for i in range(1, 4):
            total = total + y_in[h, i].astype(jnp.float32)
        half[h] = total
        last.append(remote(half.at[h], half_in.at[h], h_send.at[h], h_recv.at[h], partner))
        out_self[:, ours(h)] = half[h, 0]
        out_neigh[:, ours(h)] = half[h, 1]
    for h in range(2):
        last[h].wait_recv()
        out_self[:, theirs(h)] = half_in[h, 0]
        out_neigh[:, theirs(h)] = half_in[h, 1]
    for copy in [*pairs, *started.values(), *across.values(), *last]:
        copy.wait_send()
    for i, j in others:
        by_peer(feat_peer(i, j), lambda: whole(i, j).wait_send(), lambda: sent_late(i, j))


def layer(count, first, x, helped, w_half, bias, cot):
    block, rows = x.shape[2], cot.shape[0]
    half_wide, hidden = w_half.shape
    quarter = hidden // 4
    bf16, f32 = jnp.bfloat16, jnp.float32
    vmem = pl.BlockSpec(memory_space=pltpu.VMEM)
    hbm = pl.BlockSpec(memory_space=pl.ANY)
    dma = pltpu.SemaphoreType.DMA
    return pl.pallas_call(
        layer_kernel,
        in_specs=[pl.BlockSpec(memory_space=pltpu.SMEM), hbm, hbm, hbm, hbm, vmem, vmem],
        out_specs=[vmem, vmem, vmem],
        out_shape=[
            jax.ShapeDtypeStruct((rows, hidden), bf16),
            jax.ShapeDtypeStruct((block, hidden), f32),
            jax.ShapeDtypeStruct((block, hidden), f32),
        ],
        scratch_shapes=[
            pltpu.VMEM((2 * half_wide, hidden), bf16),
            pltpu.VMEM((2, half_wide, rows), bf16),
            pltpu.VMEM((SHARED, 2, block, rows // 3), bf16),
            pltpu.VMEM((SHARED, 2, block, rows // 3), bf16),
            pltpu.VMEM((rows, 2 * half_wide), bf16),
            pltpu.VMEM((rows, hidden), bf16),
            pltpu.VMEM((4, half_wide, quarter), bf16),
            pltpu.VMEM((4, half_wide, quarter), bf16),
            pltpu.VMEM((2, 4, 2, 4, block, quarter), bf16),
            pltpu.VMEM((2, 3, 2, 4, block, quarter), bf16),
            pltpu.VMEM((2, 4, 2, block, quarter), bf16),
            pltpu.VMEM((2, 3, 2, block, quarter), bf16),
            pltpu.VMEM((2, 4, 2, block, quarter), bf16),
            pltpu.VMEM((2, 2, block, quarter), f32),
            pltpu.VMEM((2, 2, block, quarter), f32),
            dma((16,)), dma((16,)), dma((4,)), dma((4,)), dma((2, 2, 6)), dma((2, 2, 6)),
            dma((2, 4)), dma((2, 4)), dma((2,)), dma((2,)), dma((3,)), dma((3,)), dma((3,)),
            dma((16,)), dma((16,)),
        ],
        compiler_params=pltpu.CompilerParams(
            collective_id=0, has_side_effects=True, vmem_limit_bytes=56 << 20
        ),
        cost_estimate=pl.CostEstimate(
            flops=2_500_000_000, bytes_accessed=10_000_000, transcendentals=0
        ),
    )(count, first, x, helped, w_half, bias, cot)


def local(node_table, neighbor_ids, tile_counts, w_self, w_neigh, bias, cotangent):
    owned, rows, hidden = cotangent.shape
    ids = neighbor_ids.transpose(1, 0, 2)
    nodes, counts, first, w_half, pair_counts, pair_ids = first_tiles(
        tile_counts, ids, node_table, w_self, w_neigh
    )
    x, helped = gather(counts, pair_counts, ids, pair_ids, nodes, node_table.shape[0])
    act, grad_self, grad_neigh = layer(
        tile_counts,
        first,
        x,
        helped,
        w_half,
        bias.reshape(1, hidden),
        cotangent.reshape(owned * rows, hidden),
    )
    act, grad_self, grad_neigh = finish(act, grad_self, grad_neigh)
    return act.reshape(owned, rows, hidden), grad_self, grad_neigh


def solution(mesh):
    return jax.shard_map(
        local,
        mesh=mesh,
        in_specs=(
            P("feat", None),
            P("dp", None, None),
            P(("dp", "feat")),
            P("feat", None),
            P("feat", None),
            P(),
            P(("dp", "feat"), None, None),
        ),
        out_specs=(P(("dp", "feat"), None, None), P("feat", None), P("feat", None)),
        check_vma=False,
    )
```
